32 devices in a mesh: member: 2 (over core), tile: 16 (over z, y, x).
Axes of the slice: x: 2, y: 2, z: 4, core: 2. Of those that a mesh axis runs over, the one named last changes fastest.
Arguments:
- parent_state: float32 [4, 81, 128, 128], P('member', None, 'tile'), may hold values from -6 to 6
- nest_state: float32 [4, 81, 4096], P('member', None, 'tile'), may hold values from -6 to 6
- terrain: int32 [128, 128], P('tile'), may hold values from 0 to 3000
- shift_x: int32 [4], replicated, may hold values from -16 to 16
- boundary_index: int32 [4, 256], P(None, 'tile'), may hold values from 0 to 16383, as said below
- reloc_dest: int32 [4, 4096], P(None, 'tile'), may hold values from 0 to 4095, as said below
Outputs:
- parent_out: float32 [4, 81, 128, 128], P('member', None, 'tile')
- nest_out: float32 [4, 81, 4096], P('member', None, 'tile')
- nest_mean: float32 [81, 4096], P(None, 'tile')
- nest_variance: float32 [81, 4096], P(None, 'tile')
The draws below stay inside these ranges and needn't reach their ends.
Inputs may be any that keep to these rules, and one draw needn't show every extreme that they name: `boundary_index`: for each step and nest tile t, entries t * 16 to t * 16 + 15 come in 8 runs of 2; each run lies on one parent tile (rows of 8), different runs of one tile on different parent tiles, and the cells within one run differ. `reloc_dest`: for each step a permutation of the 4096 nest columns. The columns of one tile go in runs of 32 (slots g * 32 to g * 32 + 31) each wholly to one tile, into that tile's run g; the runs of one tile go to 8 different tiles, so exactly 32 or no columns pass from one tile to another.
All inputs are finite; a program needn't handle non-finite values.
Results may differ from the reference program's by a relative error of at most 0.00047.
Values may be sent and summed in bfloat16 or wider, within the bound.
A program may use at most 64 MiB of HBM per device.

```python
import jax
import jax.numpy as jnp

LEV = 81
PY_DEV = 8
PXW = 128
NC_DEV = 256
CAPB = 2
STEPS = 4
MEMBERS = 4
NPY = 128
CELLS = 1024
NCOLS = 4096
GROUPS = 8
CAP = 32
OWNERS = 8
NB_DEV = 16
N_TILE = 16


def draw_boundary_index(key, part):
    tile_count = NPY // PY_DEV
    pieces = []
    for step_no in range(STEPS):
        step_key = jax.random.fold_in(jax.random.fold_in(key, 11), step_no)
        key_start, key_jitter = jax.random.split(step_key, 2)
        starts = jax.random.randint(key_start, (tile_count, 1, 1), 0, max(tile_count // 4, 1))
        starts = starts.at[0, 0, 0].set(tile_count - OWNERS)
        starts = starts.at[1, 0, 0].set(0)
        run_index = jnp.arange(OWNERS, dtype=jnp.int32).reshape(1, OWNERS, 1)
        owner_tile = (starts + run_index) % tile_count
        stride = CELLS // CAPB
        jitter = jax.random.randint(key_jitter, (tile_count, OWNERS, CAPB), 0, stride)
        jitter = jitter.at[0, OWNERS - 1, CAPB - 1].set(stride - 1)
        jitter = jitter.at[1, 0, 0].set(0)
        within = jnp.arange(CAPB, dtype=jnp.int32).reshape(1, 1, CAPB) * stride + jitter
        pieces.append((owner_tile * CELLS + within).reshape(-1))
    return jnp.stack(pieces, axis=0).astype(jnp.int32)


def draw_reloc_dest(key, part):
    tile_count = NPY // PY_DEV
    pieces = []
    for step_no in range(STEPS):
        step_key = jax.random.fold_in(jax.random.fold_in(key, 23), step_no)
        key_order, key_offset, key_slots = jax.random.split(step_key, 3)
        order = jax.random.permutation(key_order, tile_count).astype(jnp.int32)
        inverse = jnp.argsort(order).astype(jnp.int32)
        offsets = jax.random.permutation(key_offset, tile_count)[:GROUPS].astype(jnp.int32)
        sources = jnp.arange(tile_count, dtype=jnp.int32)
        target_tile = order[(inverse[sources][:, None] + offsets[None, :]) % tile_count]
        scores = jax.random.randint(key_slots, (tile_count, GROUPS, CAP), 0, 1 << 20) * CAP
        scores = scores + jnp.arange(CAP, dtype=jnp.int32).reshape(1, 1, CAP)
        within = jnp.argsort(scores, axis=-1, stable=True).astype(jnp.int32)
        group_base = jnp.arange(GROUPS, dtype=jnp.int32).reshape(1, GROUPS, 1) * CAP
        targets = target_tile[:, :, None] * NC_DEV + group_base + within
        pieces.append(targets.reshape(-1))
    return jnp.stack(pieces, axis=0).astype(jnp.int32)


def plant(values, key, smallest, top_value):
    place = [jax.random.randint(jax.random.fold_in(key, axis), (), 0, length) for axis, length in enumerate(values.shape)]
    main_axis = values.shape.index(max(values.shape))
    beside = place[:main_axis] + [(place[main_axis] + 1) % values.shape[main_axis]] + place[main_axis + 1:]
    return values.at[tuple(place)].set(smallest).at[tuple(beside)].set(top_value)


def block_levels(own_key, extent, cuts, smallest, high):
    level, own = 1.0, jax.random.fold_in(own_key, 6)
    for dim, shards_of in cuts:
        draws = jnp.exp(jax.random.uniform(jax.random.fold_in(own, dim), (shards_of,), jnp.float32, smallest / len(cuts), high / len(cuts)))
        level = level * jnp.repeat(draws, extent[dim] // shards_of).reshape([-1 if axis == dim else 1 for axis in range(len(extent))])
    return level


def bell_draw(own_key, extent, scale, bound, shards=(), kind=jnp.bfloat16):
    values = scale * jax.random.normal(own_key, extent, jnp.float32)
    if shards:
        values = values * block_levels(own_key, extent, shards, -0.22, 0.18)
    return jnp.clip(values, -bound, bound).astype(kind)


def setup_inputs(seed: int = 0) -> dict:
    splits = jax.random.split(jax.random.key(seed), 7)
    return {
        "parent_state": bell_draw(splits[0], (MEMBERS, LEV, NPY, PXW), 1.0, 6.0, ((0, 2), (2, 16)), jnp.float32),
        "nest_state": bell_draw(splits[1], (MEMBERS, LEV, NCOLS), 1.0, 6.0, ((0, 2), (2, 16)), jnp.float32),
        "terrain": plant(jax.random.randint(splits[2], (NPY, PXW), 0, 3001), jax.random.fold_in(splits[2], 1), 0, 3000).astype(jnp.int32),
        "shift_x": plant(jax.random.randint(splits[3], (STEPS,), -16, 17), jax.random.fold_in(splits[3], 1), -16, 16).astype(jnp.int32),
        "boundary_index": draw_boundary_index(jax.random.fold_in(splits[6], 71), 0),
        "reloc_dest": draw_reloc_dest(jax.random.fold_in(splits[6], 71), 0),
    }


HORIZ_MIX = 0.15
VERT_MIX = 0.1
DRAG_RATE = 0.1
RELAX_RATE = 0.5
IMPLICIT_MIX = 0.8


def parent_update(parent, damping):
    padded = jnp.pad(parent, ((0, 0), (0, 0), (1, 1), (0, 0)))
    north_row = padded[:, :, 2:, :]
    south_row = padded[:, :, :-2, :]
    east_cell = jnp.roll(parent, -1, axis=3)
    west_cell = jnp.roll(parent, 1, axis=3)
    upper_level = jnp.concatenate([parent[:, 1:], parent[:, -1:]], axis=1)
    lower_level = jnp.concatenate([parent[:, :1], parent[:, :-1]], axis=1)
    return (parent + HORIZ_MIX * (north_row + south_row + east_cell + west_cell - 4.0 * parent)
            + VERT_MIX * (upper_level + lower_level - 2.0 * parent) - damping * parent)


def implicit_column(column_field):
    levels = column_field.shape[1]
    pivots = []
    cprime = []
    previous = 0.0
    for level in range(levels):
        neighbours = (1 if level > 0 else 0) + (1 if level < levels - 1 else 0)
        diagonal = 1.0 + IMPLICIT_MIX * neighbours
        pivot = diagonal - IMPLICIT_MIX * previous if level > 0 else diagonal
        previous = IMPLICIT_MIX / pivot
        pivots.append(pivot)
        cprime.append(previous)
    sweep = []
    forward = None
    for level in range(levels):
        source = column_field[:, level]
        if level > 0:
            source = source + IMPLICIT_MIX * forward
        forward = source / pivots[level]
        sweep.append(forward)
    result = [None] * levels
    result[levels - 1] = sweep[levels - 1]
    for level in range(levels - 2, -1, -1):
        result[level] = sweep[level] + cprime[level] * result[level + 1]
    return jnp.stack(result, axis=1)


def reference(parent_state, nest_state, terrain, shift_x, boundary_index, reloc_dest):
    damping = DRAG_RATE * terrain.astype(jnp.float32) / 3000.0
    parent = parent_state
    nest_field = nest_state
    members, levels, ncols = nest_field.shape
    for step_no in range(STEPS):
        flat_parent = parent.astype(jnp.bfloat16).reshape(members, levels, -1)
        indices = boundary_index[step_no]
        rows_at = indices // PXW
        cols_at = jnp.mod(indices % PXW + shift_x[step_no], PXW)
        picked = jnp.take(flat_parent, rows_at * PXW + cols_at, axis=2).astype(jnp.float32)
        picked = picked.reshape(members, levels, N_TILE, NB_DEV)
        blocks = nest_field.reshape(members, levels, N_TILE, NC_DEV)
        edge_cols = blocks[..., :NB_DEV]
        edge_cols = edge_cols + RELAX_RATE * (picked - edge_cols)
        blocks = jnp.concatenate([edge_cols, blocks[..., NB_DEV:]], axis=3)
        nest_field = implicit_column(blocks.reshape(members, levels, ncols))
        nest_field = jnp.zeros_like(nest_field).at[:, :, reloc_dest[step_no]].set(nest_field)
        parent = parent_update(parent, damping)
    mean_field = jnp.sum(nest_field, axis=0) / MEMBERS
    variance = jnp.sum((nest_field - mean_field) ** 2, axis=0) / MEMBERS
    return parent, nest_field, mean_field, variance
```

```python
import functools

import jax
import jax.numpy as jnp
import numpy as np
from jax import lax
from jax.experimental import pallas as pl
from jax.experimental.pallas import tpu as pltpu
from jax.sharding import PartitionSpec as P

CAPB = 2
STEPS = 4


HORIZ_MIX = 0.15
VERT_MIX = 0.1
DRAG_RATE = 0.1
RELAX_RATE = 0.5
IMPLICIT_MIX = 0.8


def with_halo(block, sides, width):
    for axis, dim in sides:
        count = lax.axis_size(axis)
        forward = [(i, i + 1) for i in range(count - 1)]
        backward = [(target, source) for source, target in forward]
        low = lax.ppermute(
            lax.slice_in_dim(block, block.shape[dim] - width, None, axis=dim), axis, forward
        )
        high = lax.ppermute(lax.slice_in_dim(block, 0, width, axis=dim), axis, backward)
        block = jnp.concatenate([low, block, high], axis=dim)
    return block


def parent_update(parent, damping):
    padded = with_halo(parent, (("tile", 2),), 1)
    north_row = padded[:, :, 2:, :]
    south_row = padded[:, :, :-2, :]
    east_cell = jnp.roll(parent, -1, axis=3)
    west_cell = jnp.roll(parent, 1, axis=3)
    upper_level = jnp.concatenate([parent[:, 1:], parent[:, -1:]], axis=1)
    lower_level = jnp.concatenate([parent[:, :1], parent[:, :-1]], axis=1)
    return (
        parent
        + HORIZ_MIX * (north_row + south_row + east_cell + west_cell - 4.0 * parent)
        + VERT_MIX * (upper_level + lower_level - 2.0 * parent)
        - damping * parent
    )


def implicit_column(column_field):
    levels = column_field.shape[1]
    pivots = []
    cprime = []
    previous = 0.0
    for level in range(levels):
        neighbours = (1 if level > 0 else 0) + (1 if level < levels - 1 else 0)
        diagonal = 1.0 + IMPLICIT_MIX * neighbours
        pivot = diagonal - IMPLICIT_MIX * previous if level > 0 else diagonal
        previous = IMPLICIT_MIX / pivot
        pivots.append(pivot)
        cprime.append(previous)
    sweep = []
    forward = None
    for level in range(levels):
        source = column_field[:, level]
        if level > 0:
            source = source + IMPLICIT_MIX * forward
        forward = source / pivots[level]
        sweep.append(forward)
    result = [None] * levels
    result[levels - 1] = sweep[levels - 1]
    for level in range(levels - 2, -1, -1):
        result[level] = sweep[level] + cprime[level] * result[level + 1]
    return jnp.stack(result, axis=1)


def locate(indices, shift_by, row_width, tile_cells):
    rows_at = indices // row_width
    cols_at = jnp.mod(indices % row_width + shift_by, row_width)
    moved = rows_at * row_width + cols_at
    return (moved // tile_cells, moved % tile_cells)


def on_device(parent_state, nest_state, terrain, shift_x, boundary_index, reloc_dest):
    members, levels, rows_here, row_width = parent_state.shape
    columns_here = nest_state.shape[2]
    tile_count = lax.axis_size("tile")
    tile_cells = rows_here * row_width
    boundary_here = boundary_index.shape[1]
    owners = boundary_here // CAPB
    mixed = members * levels
    groups = tile_count // 2
    per_peer = columns_here // groups
    damping = DRAG_RATE * terrain.astype(jnp.float32) / 3000.0
    parent = parent_state
    nest_field = nest_state
    for step_no in range(STEPS):
        flat_parent = parent.astype(jnp.bfloat16).reshape(mixed, tile_cells)
        offset = shift_x[step_no]
        owner_of, local_of = locate(boundary_index[step_no], offset, row_width, tile_cells)
        owner_runs = owner_of.reshape(owners, CAPB)[:, 0]
        local_runs = local_of.reshape(owners, CAPB)
        requests_out = jnp.zeros((tile_count, CAPB), jnp.int32).at[owner_runs].set(local_runs)
        values = jnp.transpose(
            jnp.take(
                flat_parent,
                lax.all_to_all(requests_out, "tile", split_axis=0, concat_axis=0, tiled=True),
                axis=1,
            ),
            (1, 2, 0),
        )
        received = lax.all_to_all(values, "tile", split_axis=0, concat_axis=0, tiled=True)
        edge_values = received[owner_runs].reshape(boundary_here, mixed)
        edge_values = (
            jnp.transpose(edge_values).astype(jnp.float32).reshape(members, levels, boundary_here)
        )
        edge_cols = nest_field[:, :, :boundary_here]
        edge_cols = edge_cols + RELAX_RATE * (edge_values - edge_cols)
        nest_field = jnp.concatenate([edge_cols, nest_field[:, :, boundary_here:]], axis=2)
        nest_field = implicit_column(nest_field)
        targets = reloc_dest[step_no].reshape(groups, per_peer)
        target_tile = targets[:, 0] // columns_here
        slots = targets % columns_here
        values_out = jnp.transpose(nest_field.reshape(mixed, groups, per_peer), (1, 2, 0))
        send_values = (
            jnp.zeros((tile_count, per_peer, mixed), jnp.float32).at[target_tile].set(values_out)
        )
        send_slots = (
            jnp.full((tile_count, per_peer), columns_here, jnp.int32).at[target_tile].set(slots)
        )
        got_values, got_slots = (
            lax.all_to_all(send_values, "tile", split_axis=0, concat_axis=0, tiled=True),
            lax.all_to_all(send_slots, "tile", split_axis=0, concat_axis=0, tiled=True),
        )
        placed = (
            jnp.zeros((columns_here, mixed), jnp.float32)
            .at[got_slots.reshape(-1)]
            .set(got_values.reshape(-1, mixed), mode="drop")
        )
        nest_field = jnp.transpose(placed).reshape(members, levels, columns_here)
        parent = parent_update(parent, damping)
    ensemble = members * lax.axis_size("member")
    totals = lax.psum(jnp.sum(nest_field, axis=0), "member")
    mean_field = totals / ensemble
    spread_sum = lax.psum(jnp.sum((nest_field - mean_field) ** 2, axis=0), "member")
    variance = spread_sum / ensemble
    return (parent, nest_field, mean_field, variance)


MESH = pl.DeviceIdType.MESH
F32 = jnp.float32
BF16 = jnp.bfloat16
HI = lax.Precision.HIGHEST
PLANE = 4
LANES = 128


def inverse_powers(levels):
    a = np.zeros((levels, levels))
    for level in range(levels):
        a[level, level] = 1.0
        for other in (level - 1, level + 1):
            if 0 <= other < levels:
                a[level, level] += IMPLICIT_MIX
                a[level, other] = -IMPLICIT_MIX
    inv = np.linalg.inv(a)
    out = np.zeros((STEPS, LANES, LANES), np.float32)
    power = np.eye(levels)
    for k in range(STEPS):
        power = power @ inv
        out[k, :levels, :levels] = power
    return out


def nn(a, b, precision=None):
    return lax.dot_general(
        a, b, (((1,), (0,)), ((), ())), preferred_element_type=F32, precision=precision
    )


def nt(a, b, precision=None):
    return lax.dot_general(
        a, b, (((1,), (1,)), ((), ())), preferred_element_type=F32, precision=precision
    )


def one_hot(mask):
    return jnp.where(mask, 1.0, 0.0).astype(BF16)


def fused(
    dims,
    parent_ref, nest_ref, terrain_ref, shift_ref, bound_ref, dest_ref, inv_ref,
    parent_out, nest_out, mean_out, var_out,
    meta, halo_out, halo_in, terr_in, zg, pm, pr, w, msg, got, mine, theirs,
    meta_s, meta_r, halo_s, halo_r, terr_s, terr_r, z_s, z_r, p_s, p_r, msg_s, msg_r, mem_s, mem_r,
):
    members, levels, rows, width, cols, nb, tiles, per, cells = dims
    padded = zg.shape[2]
    zs = tiles // PLANE
    tall = 2 * rows
    half = rows // 2
    me = lax.axis_index("tile")
    core = lax.axis_index("member")
    my_p = lax.rem(me, PLANE)
    my_z = me // PLANE

    def rcopy(src, dst, ssem, rsem, tile, member=None):
        return pltpu.make_async_remote_copy(
            src_ref=src, dst_ref=dst, send_sem=ssem, recv_sem=rsem,
            device_id=(core if member is None else member, tile), device_id_type=MESH,
        )

    def at(d):
        return lax.rem(me + d, tiles)

    barrier = pltpu.get_barrier_semaphore()
    for d in range(1, tiles):
        pl.semaphore_signal(barrier, inc=1, device_id=(core, at(d)), device_id_type=MESH)
    pl.semaphore_signal(barrier, inc=1, device_id=(1 - core, me), device_id_type=MESH)

    row_i = lax.broadcasted_iota(jnp.int32, (rows, width), 0)

    def pack(level, _):
        p0 = parent_ref[level]
        p1 = parent_ref[levels + level]
        halo_out[0, level] = jnp.where(row_i < half, pltpu.roll(p0, half, axis=0), p1)
        halo_out[1, level] = jnp.where(row_i < half, p0, pltpu.roll(p1, half, axis=0))
        return 0

    lax.fori_loop(0, levels, pack, 0)

    meta[me, 0:STEPS, :] = dest_ref[...]
    meta[me, STEPS : 2 * STEPS, :] = jnp.zeros((STEPS, cols), jnp.int32)
    for s in range(STEPS):
        index = bound_ref[s : s + 1, :]
        at_col = lax.rem(lax.rem(index, width) + shift_ref[s] + width, width)
        meta[me, STEPS + s : STEPS + s + 1, 0:nb] = (index // width) * width + at_col

    last = inv_ref[STEPS - 1][:padded, :levels]
    for m in range(members):
        zg[my_z, m] = nn(last, nest_ref[m], HI)

    pl.semaphore_wait(barrier, tiles)

    pending = []

    def start(copy):
        copy.start()
        pending.append(copy)

    for d in range(1, tiles):
        start(rcopy(meta.at[me], meta.at[me], meta_s.at[d], meta_r.at[d], at(d)))

    def halo_pair(i, tile):
        return (
            rcopy(halo_out.at[i], halo_in.at[i], halo_s.at[i], halo_r.at[i], tile),
            rcopy(terrain_ref, terr_in.at[i], terr_s.at[i], terr_r.at[i], tile),
        )

    has = (me < tiles - 1, me > 0)
    to = (lax.rem(me + 1, tiles), lax.rem(me + tiles - 1, tiles))
    for i in range(2):
        @pl.when(has[i])
        def _():
            for copy in halo_pair(i, to[i]):
                copy.start()

    for d in range(1, zs):
        start(rcopy(zg.at[my_z], zg.at[my_z], z_s.at[d], z_r.at[d], at(d * PLANE)))

    for d in range(1, tiles):
        rcopy(meta.at[me], meta.at[at(tiles - d)], meta_s.at[d], meta_r.at[d], me).wait_recv()

    t_iota = lax.broadcasted_iota(jnp.int32, (tiles, cols), 0)
    dest = [meta[:, s, :] for s in range(STEPS)]
    dest_tile = [v // cols for v in dest]

    def chase(final):
        tau = jnp.zeros((1, cols), jnp.int32) + final
        sources, slots, firsts = [None] * STEPS, [None] * STEPS, [None] * STEPS
        for s in range(STEPS - 1, -1, -1):
            hit = dest_tile[s] == tau
            tau = jnp.sum(jnp.where(hit, t_iota, 0), axis=0, keepdims=True)
            slots[s] = jnp.sum(jnp.where(hit, dest[s] - dest_tile[s] * cols, 0), axis=0, keepdims=True)
            sources[s] = tau
        return sources, slots

    lane_t = lax.broadcasted_iota(jnp.int32, (tiles, LANES), 1)
    lane_c = lax.broadcasted_iota(jnp.int32, (tiles, cols), 1)
    cell_iota = lax.broadcasted_iota(jnp.int32, (tiles, cells), 1)
    eye = one_hot(lax.broadcasted_iota(jnp.int32, (LANES, LANES), 0)
                  == lax.broadcasted_iota(jnp.int32, (LANES, LANES), 1))
    requests = [None] * STEPS
    path = None
    for s in range(STEPS - 1, -1, -1):
        hop = one_hot(dest_tile[s][:, 0:1] == lane_t)
        hop = jnp.concatenate([hop, jnp.zeros((LANES - tiles, LANES), BF16)], axis=0)
        path = hop if path is None else nn(hop, path).astype(BF16)
        back = nt(eye, path).astype(BF16)[0:tiles, :]
        cell = meta[:, STEPS + s, :]
        owned = jnp.logical_and(cell // cells == me, lane_c < nb)
        local = lax.rem(cell, cells) + 1
        parts = []
        for k in range(CAPB):
            pick = jnp.logical_and(owned, lax.rem(lane_c, CAPB) == k)
            which = jnp.sum(jnp.where(pick, local, 0), axis=1, keepdims=True) - 1
            asked = one_hot(cell_iota == which)
            asked = jnp.concatenate([asked, jnp.zeros((LANES - tiles, cells), BF16)], axis=0)
            parts.append(nn(back, asked).astype(BF16))
        requests[s] = jnp.concatenate(parts, axis=0)

    sources, slots = chase(me)

    q_iota = lax.broadcasted_iota(jnp.int32, (cols, cols), 0)
    j_iota = lax.broadcasted_iota(jnp.int32, (cols, cols), 1)
    relax = jnp.where(j_iota < nb, 1.0 - RELAX_RATE, 1.0)
    moves = [None] * STEPS
    path = None
    for s in range(STEPS - 1, -1, -1):
        hop = jnp.where(slots[s] == q_iota, relax, 0.0).astype(BF16)
        path = hop if path is None else nn(path, hop).astype(BF16)
        moves[s] = path

    for d in range(1, zs):
        rcopy(
            zg.at[my_z], zg.at[lax.rem(my_z + zs - d, zs)], z_s.at[d], z_r.at[d], me
        ).wait_recv()

    def masked(origin, m):
        out = jnp.zeros((padded, cols), F32)
        for z in range(zs):
            out = jnp.where(origin == z * PLANE + my_p, zg[z, m], out)
        return out

    for d in range(1, PLANE):
        final = my_z * PLANE + lax.rem(my_p + d, PLANE)
        origin = chase(final)[0][0]
        for m in range(members):
            pm[d - 1, m] = masked(origin, m)
        start(rcopy(pm.at[d - 1], pr.at[d - 1], p_s.at[d], p_r.at[d], final))

    for i in range(2):
        @pl.when(has[1 - i])
        def _():
            for copy in halo_pair(i, me):
                copy.wait_recv()

        @pl.when(jnp.logical_not(has[1 - i]))
        def _():
            halo_in[i] = jnp.zeros((levels, rows, width), F32)
            terr_in[i] = jnp.zeros((rows, width), jnp.int32)

    row_t = lax.broadcasted_iota(jnp.int32, (tall, width), 0) + me * rows - half
    inside = jnp.logical_and(row_t >= 0, row_t < tiles * rows)

    def fill(level, _):
        low = halo_in[0, level]
        high = halo_in[1, level]
        for m in range(members):
            base = pl.multiple_of((m * levels + level) * tall, tall)
            own = pltpu.roll(parent_ref[m * levels + level], half, axis=0)
            lo = low if m == 0 else pltpu.roll(low, half, axis=0)
            hi = pltpu.roll(high, half, axis=0) if m == 0 else high
            top = jnp.where(row_i < half, lo, own)
            bottom = jnp.where(row_i < half, own, hi)
            w[pl.ds(base, tall), :] = jnp.concatenate([top, bottom], axis=0)
        return 0

    lax.fori_loop(0, levels, fill, 0)
    tail = members * levels * tall
    w[tail:, :] = jnp.zeros((w.shape[0] - tail, width), F32)

    terr = terrain_ref[...]
    terr_own = pltpu.roll(terr, half, axis=0)
    terr_all = jnp.concatenate(
        [
            jnp.where(row_i < half, pltpu.roll(terr_in[0], half, axis=0), terr_own),
            jnp.where(row_i < half, terr_own, pltpu.roll(terr_in[1], half, axis=0)),
        ],
        axis=0,
    )
    damping = DRAG_RATE * terr_all.astype(F32) / 3000.0
    centre = 1.0 - 4.0 * HORIZ_MIX - 2.0 * VERT_MIX - damping

    chunk = 9 if levels % 9 == 0 else 1

    def advance(final):
        def body(c, before):
            before = list(before)
            for u in range(chunk):
                level = c * chunk + u
                for m in range(members):
                    base = pl.multiple_of((m * levels + level) * tall, tall)
                    above = pl.multiple_of(
                        (m * levels + jnp.minimum(level + 1, levels - 1)) * tall, tall
                    )
                    cur = w[pl.ds(base, tall), :]
                    up = w[pl.ds(above, tall), :]
                    sides = (
                        pltpu.roll(cur, 1, axis=0) + pltpu.roll(cur, tall - 1, axis=0)
                        + pltpu.roll(cur, 1, axis=1) + pltpu.roll(cur, width - 1, axis=1)
                    )
                    new = centre * cur + HORIZ_MIX * sides + VERT_MIX * (up + before[m])
                    if final:
                        parent_out[m * levels + level] = new[half : half + rows]
                    else:
                        w[pl.ds(base, tall), :] = jnp.where(inside, new, 0.0)
                    before[m] = cur
            return tuple(before)

        first = tuple(w[m * levels * tall : (m * levels + 1) * tall, :] for m in range(members))
        lax.fori_loop(0, levels // chunk, body, first)

    slot_rows = members * STEPS * CAPB

    def pick(s):
        for m in range(members):
            pieces = [
                w[pl.ds(m * levels * tall + half + r, padded, stride=tall), :] for r in range(rows)
            ]
            field = jnp.concatenate(pieces, axis=1)
            field = jnp.concatenate([field, jnp.zeros((LANES - padded, cells), F32)], axis=0)
            values = nt(requests[s], field.astype(BF16))
            for k in range(CAPB):
                slot = m * STEPS * CAPB + s * CAPB + k
                msg[pl.ds(slot, tiles, stride=slot_rows), :] = values[k * tiles : (k + 1) * tiles]

    for s in range(STEPS - 1):
        pick(s)
        advance(False)
    pick(STEPS - 1)

    def rows_of(tile):
        return pl.ds(pl.multiple_of(tile * slot_rows, slot_rows), slot_rows)

    for d in range(1, tiles):
        start(rcopy(msg.at[rows_of(at(d))], got.at[rows_of(me)], msg_s.at[d], msg_r.at[d], at(d)))
    got[rows_of(me), :] = msg[rows_of(me), :]

    advance(True)

    origin = sources[0]
    for d in range(1, PLANE):
        rcopy(pm.at[d - 1], pr.at[d - 1], p_s.at[d], p_r.at[d], me).wait_recv()
    result = []
    for m in range(members):
        block = masked(origin, m)
        for d in range(1, PLANE):
            came = lax.rem(origin, PLANE) == lax.rem(my_p + PLANE - d, PLANE)
            block = jnp.where(came, pr[d - 1, m], block)
        result.append(nt(block, moves[0].astype(F32), HI))

    g_rows = tiles * slot_rows
    g_iota = lax.broadcasted_iota(jnp.int32, (g_rows, cols), 0)
    g_lane = lax.broadcasted_iota(jnp.int32, (g_rows, cols), 1)
    g_owner = g_iota // slot_rows
    g_slot = lax.rem(g_iota, slot_rows)
    takes = [[None] * STEPS for _ in range(members)]
    for s in range(STEPS):
        asker = sources[s][:, 0:1]
        cell = jnp.sum(
            jnp.where(t_iota == asker, meta[:, STEPS + s, :], 0), axis=0, keepdims=True
        )
        ours = jnp.logical_and(g_owner == cell // cells, g_lane < nb)
        for m in range(members):
            slot = m * STEPS * CAPB + s * CAPB + lax.rem(g_lane, CAPB)
            takes[m][s] = nt(
                one_hot(jnp.logical_and(ours, g_slot == slot)), moves[s]
            ).astype(BF16)

    for d in range(1, tiles):
        rcopy(
            msg.at[rows_of(me)], got.at[rows_of(at(tiles - d))], msg_s.at[d], msg_r.at[d], me
        ).wait_recv()
    arrived = jnp.transpose(got[...]).astype(BF16)
    for m in range(members):
        for s in range(STEPS):
            entry = nn(arrived, takes[m][s])
            result[m] = result[m] + nn(inv_ref[STEPS - 1 - s], entry, HI)[:padded]
        mine[m] = result[m]
        nest_out[m] = result[m][:levels]

    pair = rcopy(mine, theirs, mem_s, mem_r, me, 1 - core)
    pair.start()
    pair.wait()
    count = 2 * members
    fields = [mine[m, 0:levels] for m in range(members)]
    fields += [theirs[m, 0:levels] for m in range(members)]
    mean = functools.reduce(lambda a, b: a + b, fields) / count
    mean_out[...] = mean
    var_out[...] = functools.reduce(lambda a, b: a + b, [(f - mean) ** 2 for f in fields]) / count

    for copy in pending:
        copy.wait_send()
    for i in range(2):
        @pl.when(has[i])
        def _():
            for copy in halo_pair(i, to[i]):
                copy.wait_send()


def on_device_fused(parent_state, nest_state, terrain, shift_x, boundary_index, reloc_dest):
    members, levels, rows, width = parent_state.shape
    cols = nest_state.shape[2]
    nb = boundary_index.shape[1]
    tiles = lax.axis_size("tile")
    cells = rows * width
    padded = -(-levels // 8) * 8
    zs = tiles // PLANE
    slot_rows = members * STEPS * CAPB
    dims = (members, levels, rows, width, cols, nb, tiles, cols // (tiles // 2), cells)
    vmem = pl.BlockSpec(memory_space=pltpu.VMEM)
    dma = pltpu.SemaphoreType.DMA
    outs = pl.pallas_call(
        functools.partial(fused, dims),
        out_shape=(
            jax.ShapeDtypeStruct((members * levels, rows, width), F32),
            jax.ShapeDtypeStruct((members, levels, cols), F32),
            jax.ShapeDtypeStruct((levels, cols), F32),
            jax.ShapeDtypeStruct((levels, cols), F32),
        ),
        in_specs=[vmem, vmem, vmem, pl.BlockSpec(memory_space=pltpu.SMEM), vmem, vmem, vmem],
        out_specs=(vmem,) * 4,
        scratch_shapes=[
            pltpu.VMEM((tiles, 2 * STEPS, cols), jnp.int32),
            pltpu.VMEM((2, levels, rows, width), F32),
            pltpu.VMEM((2, levels, rows, width), F32),
            pltpu.VMEM((2, rows, width), jnp.int32),
            pltpu.VMEM((zs, members, padded, cols), F32),
            pltpu.VMEM((PLANE - 1, members, padded, cols), F32),
            pltpu.VMEM((PLANE - 1, members, padded, cols), F32),
            pltpu.VMEM(((members * levels + padded - levels) * 2 * rows, width), F32),
            pltpu.VMEM((tiles * slot_rows, LANES), F32),
            pltpu.VMEM((tiles * slot_rows, LANES), F32),
            pltpu.VMEM((members, padded, cols), F32),
            pltpu.VMEM((members, padded, cols), F32),
            dma((tiles,)), dma((tiles,)),
            dma((2,)), dma((2,)), dma((2,)), dma((2,)),
            dma((zs,)), dma((zs,)), dma((PLANE,)), dma((PLANE,)),
            dma((tiles,)), dma((tiles,)),
            dma, dma,
        ],
        compiler_params=pltpu.CompilerParams(
            collective_id=0, has_side_effects=True, vmem_limit_bytes=48 * 1024 * 1024
        ),
    )(
        parent_state.reshape(members * levels, rows, width),
        nest_state, terrain, shift_x, boundary_index, reloc_dest,
        jnp.asarray(inverse_powers(levels)),
    )
    return (outs[0].reshape(parent_state.shape),) + tuple(outs[1:])


def fits_one_plane_split(mesh, parent, nest, bound):
    tiles = mesh.shape["tile"]
    cols = nest[2] // tiles
    return (
        tiles == PLANE * PLANE
        and mesh.shape["member"] == 2
        and bound[1] // tiles <= cols // (tiles // 2)
        and nest[1] <= LANES
        and nest[0] == 4
        and parent[2] // tiles == 2 * STEPS
        and parent[3] == LANES
        and cols % LANES == 0
    )


def solution(mesh):
    in_specs = (
        P("member", None, "tile", None),
        P("member", None, "tile"),
        P("tile", None),
        P(),
        P(None, "tile"),
        P(None, "tile"),
    )
    out_specs = (
        P("member", None, "tile", None),
        P("member", None, "tile"),
        P(None, "tile"),
        P(None, "tile"),
    )

    def whole(parent_state, nest_state, terrain, shift_x, boundary_index, reloc_dest):
        fits = fits_one_plane_split(mesh, parent_state.shape, nest_state.shape, boundary_index.shape)
        return jax.shard_map(
            on_device_fused if fits else on_device,
            mesh=mesh, in_specs=in_specs, out_specs=out_specs, check_vma=False,
        )(parent_state, nest_state, terrain, shift_x, boundary_index, reloc_dest)

    return whole
```

```python
import functools

import jax
import jax.numpy as jnp
import numpy as np
from jax import lax
from jax.experimental import pallas as pl
from jax.experimental.pallas import tpu as pltpu
from jax.sharding import PartitionSpec as P

CAPB = 2
STEPS = 4


HORIZ_MIX = 0.15
VERT_MIX = 0.1
DRAG_RATE = 0.1
RELAX_RATE = 0.5
IMPLICIT_MIX = 0.8


def with_halo(block, sides, width):
    for axis, dim in sides:
        count = lax.axis_size(axis)
        forward = [(i, i + 1) for i in range(count - 1)]
        backward = [(target, source) for source, target in forward]
        low = lax.ppermute(
            lax.slice_in_dim(block, block.shape[dim] - width, None, axis=dim), axis, forward
        )
        high = lax.ppermute(lax.slice_in_dim(block, 0, width, axis=dim), axis, backward)
        block = jnp.concatenate([low, block, high], axis=dim)
    return block


def parent_update(parent, damping):
    padded = with_halo(parent, (("tile", 2),), 1)
    north_row = padded[:, :, 2:, :]
    south_row = padded[:, :, :-2, :]
    east_cell = jnp.roll(parent, -1, axis=3)
    west_cell = jnp.roll(parent, 1, axis=3)
    upper_level = jnp.concatenate([parent[:, 1:], parent[:, -1:]], axis=1)
    lower_level = jnp.concatenate([parent[:, :1], parent[:, :-1]], axis=1)
    return (
        parent
        + HORIZ_MIX * (north_row + south_row + east_cell + west_cell - 4.0 * parent)
        + VERT_MIX * (upper_level + lower_level - 2.0 * parent)
        - damping * parent
    )


def implicit_column(column_field):
    levels = column_field.shape[1]
    pivots = []
    cprime = []
    previous = 0.0
    for level in range(levels):
        neighbours = (1 if level > 0 else 0) + (1 if level < levels - 1 else 0)
        diagonal = 1.0 + IMPLICIT_MIX * neighbours
        pivot = diagonal - IMPLICIT_MIX * previous if level > 0 else diagonal
        previous = IMPLICIT_MIX / pivot
        pivots.append(pivot)
        cprime.append(previous)
    sweep = []
    forward = None
    for level in range(levels):
        source = column_field[:, level]
        if level > 0:
            source = source + IMPLICIT_MIX * forward
        forward = source / pivots[level]
        sweep.append(forward)
    result = [None] * levels
    result[levels - 1] = sweep[levels - 1]
    for level in range(levels - 2, -1, -1):
        result[level] = sweep[level] + cprime[level] * result[level + 1]
    return jnp.stack(result, axis=1)


def locate(indices, shift_by, row_width, tile_cells):
    rows_at = indices // row_width
    cols_at = jnp.mod(indices % row_width + shift_by, row_width)
    moved = rows_at * row_width + cols_at
    return (moved // tile_cells, moved % tile_cells)


def on_device(parent_state, nest_state, terrain, shift_x, boundary_index, reloc_dest):
    members, levels, rows_here, row_width = parent_state.shape
    columns_here = nest_state.shape[2]
    tile_count = lax.axis_size("tile")
    tile_cells = rows_here * row_width
    boundary_here = boundary_index.shape[1]
    owners = boundary_here // CAPB
    mixed = members * levels
    groups = tile_count // 2
    per_peer = columns_here // groups
    damping = DRAG_RATE * terrain.astype(jnp.float32) / 3000.0
    parent = parent_state
    nest_field = nest_state
    for step_no in range(STEPS):
        flat_parent = parent.astype(jnp.bfloat16).reshape(mixed, tile_cells)
        offset = shift_x[step_no]
        owner_of, local_of = locate(boundary_index[step_no], offset, row_width, tile_cells)
        owner_runs = owner_of.reshape(owners, CAPB)[:, 0]
        local_runs = local_of.reshape(owners, CAPB)
        requests_out = jnp.zeros((tile_count, CAPB), jnp.int32).at[owner_runs].set(local_runs)
        values = jnp.transpose(
            jnp.take(
                flat_parent,
                lax.all_to_all(requests_out, "tile", split_axis=0, concat_axis=0, tiled=True),
                axis=1,
            ),
            (1, 2, 0),
        )
        received = lax.all_to_all(values, "tile", split_axis=0, concat_axis=0, tiled=True)
        edge_values = received[owner_runs].reshape(boundary_here, mixed)
        edge_values = (
            jnp.transpose(edge_values).astype(jnp.float32).reshape(members, levels, boundary_here)
        )
        edge_cols = nest_field[:, :, :boundary_here]
        edge_cols = edge_cols + RELAX_RATE * (edge_values - edge_cols)
        nest_field = jnp.concatenate([edge_cols, nest_field[:, :, boundary_here:]], axis=2)
        nest_field = implicit_column(nest_field)
        targets = reloc_dest[step_no].reshape(groups, per_peer)
        target_tile = targets[:, 0] // columns_here
        slots = targets % columns_here
        values_out = jnp.transpose(nest_field.reshape(mixed, groups, per_peer), (1, 2, 0))
        send_values = (
            jnp.zeros((tile_count, per_peer, mixed), jnp.float32).at[target_tile].set(values_out)
        )
        send_slots = (
            jnp.full((tile_count, per_peer), columns_here, jnp.int32).at[target_tile].set(slots)
        )
        got_values, got_slots = (
            lax.all_to_all(send_values, "tile", split_axis=0, concat_axis=0, tiled=True),
            lax.all_to_all(send_slots, "tile", split_axis=0, concat_axis=0, tiled=True),
        )
        placed = (
            jnp.zeros((columns_here, mixed), jnp.float32)
            .at[got_slots.reshape(-1)]
            .set(got_values.reshape(-1, mixed), mode="drop")
        )
        nest_field = jnp.transpose(placed).reshape(members, levels, columns_here)
        parent = parent_update(parent, damping)
    ensemble = members * lax.axis_size("member")
    totals = lax.psum(jnp.sum(nest_field, axis=0), "member")
    mean_field = totals / ensemble
    spread_sum = lax.psum(jnp.sum((nest_field - mean_field) ** 2, axis=0), "member")
    variance = spread_sum / ensemble
    return (parent, nest_field, mean_field, variance)


MESH = pl.DeviceIdType.MESH
F32 = jnp.float32
BF16 = jnp.bfloat16
HI = lax.Precision.HIGHEST
PLANE = 4
LANES = 128
PARTS = 3
SUB = 16


def inverse_powers(levels):
    a = np.zeros((levels, levels))
    for level in range(levels):
        a[level, level] = 1.0
        for other in (level - 1, level + 1):
            if 0 <= other < levels:
                a[level, level] += IMPLICIT_MIX
                a[level, other] = -IMPLICIT_MIX
    inv = np.linalg.inv(a)
    padded = -(-levels // 8) * 8
    parts = np.zeros((STEPS, PARTS, padded, LANES), jnp.bfloat16)
    power = np.eye(levels)
    for k in range(STEPS):
        power = power @ inv
        rest = power
        for part in range(PARTS):
            piece = rest.astype(np.float32).astype(jnp.bfloat16)
            parts[STEPS - 1 - k, part, :levels, :levels] = piece
            rest = rest - piece.astype(np.float64)
    last = np.zeros((padded, levels), np.float32)
    last[:levels] = power
    return last, parts.reshape(STEPS * PARTS * padded, LANES)


def nn(a, b, precision=None):
    return lax.dot_general(
        a, b, (((1,), (0,)), ((), ())), preferred_element_type=F32, precision=precision
    )


def nt(a, b, precision=None):
    return lax.dot_general(
        a, b, (((1,), (1,)), ((), ())), preferred_element_type=F32, precision=precision
    )


def one_hot(mask):
    return jnp.where(mask, 1.0, 0.0).astype(BF16)


def fused(
    dims,
    parent_ref, nest_ref, terrain_ref, shift_ref, bound_ref, dest_ref, last_ref, parts_ref,
    parent_out, nest_out, mean_out, var_out,
    held, meta, halo_out, halo_in, terr_in, zg, pm, pr, w, msg, got, mine, theirs, held_s,
    meta_s, meta_r, halo_s, halo_r, terr_s, terr_r, z_s, z_r, p_s, p_r, msg_s, msg_r, mem_s, mem_r,
):
    members, levels, rows, width, cols, nb, tiles, per, cells = dims
    padded = zg.shape[2]
    zs = tiles // PLANE
    tall = 2 * rows
    half = rows // 2
    me = lax.axis_index("tile")
    core = lax.axis_index("member")
    mixed = members * levels
    tall_mixed = held.shape[0] // rows
    my_p = lax.rem(me, PLANE)
    my_z = me // PLANE

    def rcopy(src, dst, ssem, rsem, tile, member=None):
        return pltpu.make_async_remote_copy(
            src_ref=src, dst_ref=dst, send_sem=ssem, recv_sem=rsem,
            device_id=(core if member is None else member, tile), device_id_type=MESH,
        )

    def at(d):
        return lax.rem(me + d, tiles)

    barrier = pltpu.get_barrier_semaphore()
    for d in range(1, tiles):
        pl.semaphore_signal(barrier, inc=1, device_id=(core, at(d)), device_id_type=MESH)
    pl.semaphore_signal(barrier, inc=1, device_id=(1 - core, me), device_id_type=MESH)

    fetch = pltpu.make_async_copy(parent_ref, held.at[pl.ds(0, mixed * rows)], held_s)
    fetch.start()
    row_i = lax.broadcasted_iota(jnp.int32, (rows, width), 0)

    meta[me, 0:STEPS, :] = dest_ref[...]
    meta[me, STEPS : 2 * STEPS, :] = jnp.zeros((STEPS, cols), jnp.int32)
    for s in range(STEPS):
        index = bound_ref[s : s + 1, :]
        at_col = lax.rem(lax.rem(index, width) + shift_ref[s] + width, width)
        meta[me, STEPS + s : STEPS + s + 1, 0:nb] = (index // width) * width + at_col

    for m in range(members):
        zg[my_z, m] = nn(last_ref[...], nest_ref[m], HI)

    fetch.wait()
    held[mixed * rows :, :] = jnp.zeros((held.shape[0] - mixed * rows, width), F32)
    for i in range(2):
        for d in range(half):
            row = rows - 1 - d if i == 0 else d
            field = held[pl.ds(row, tall_mixed, stride=rows), :]
            near = field.astype(BF16)
            halo_out[i, d * tall_mixed : (d + 1) * tall_mixed, :] = near
            if d == 0:
                halo_out[i, half * tall_mixed :, :] = (field - near.astype(F32)).astype(BF16)

    pl.semaphore_wait(barrier, tiles)

    pending = []

    def start(copy):
        copy.start()
        pending.append(copy)

    for d in range(1, tiles):
        start(rcopy(meta.at[me], meta.at[me], meta_s.at[d], meta_r.at[d], at(d)))

    def halo_pair(i, tile):
        return (
            rcopy(halo_out.at[i], halo_in.at[i], halo_s.at[i], halo_r.at[i], tile),
            rcopy(terrain_ref, terr_in.at[i], terr_s.at[i], terr_r.at[i], tile),
        )

    has = (me < tiles - 1, me > 0)
    to = (lax.rem(me + 1, tiles), lax.rem(me + tiles - 1, tiles))
    for i in range(2):
        @pl.when(has[i])
        def _():
            for copy in halo_pair(i, to[i]):
                copy.start()

    for d in range(1, zs):
        start(rcopy(zg.at[my_z], zg.at[my_z], z_s.at[d], z_r.at[d], at(d * PLANE)))

    for d in range(1, tiles):
        rcopy(meta.at[me], meta.at[at(tiles - d)], meta_s.at[d], meta_r.at[d], me).wait_recv()

    t_iota = lax.broadcasted_iota(jnp.int32, (tiles, cols), 0)
    dest = [meta[:, s, :] for s in range(STEPS)]
    dest_tile = [v // cols for v in dest]

    def chase(final):
        tau = jnp.zeros((1, cols), jnp.int32) + final
        sources, slots, firsts = [None] * STEPS, [None] * STEPS, [None] * STEPS
        for s in range(STEPS - 1, -1, -1):
            hit = dest_tile[s] == tau
            tau = jnp.sum(jnp.where(hit, t_iota, 0), axis=0, keepdims=True)
            slots[s] = jnp.sum(jnp.where(hit, dest[s] - dest_tile[s] * cols, 0), axis=0, keepdims=True)
            sources[s] = tau
        return sources, slots

    lane_t = lax.broadcasted_iota(jnp.int32, (tiles, LANES), 1)
    lane_c = lax.broadcasted_iota(jnp.int32, (tiles, cols), 1)
    cell_iota = lax.broadcasted_iota(jnp.int32, (tiles, cells), 1)
    eye = one_hot(lax.broadcasted_iota(jnp.int32, (LANES, LANES), 0)
                  == lax.broadcasted_iota(jnp.int32, (LANES, LANES), 1))
    requests = [None] * STEPS
    path = None
    for s in range(STEPS - 1, -1, -1):
        hop = one_hot(dest_tile[s][:, 0:1] == lane_t)
        hop = jnp.concatenate([hop, jnp.zeros((LANES - tiles, LANES), BF16)], axis=0)
        path = hop if path is None else nn(hop, path).astype(BF16)
        back = nt(eye, path).astype(BF16)[0:tiles, :]
        cell = meta[:, STEPS + s, :]
        owned = jnp.logical_and(cell // cells == me, lane_c < nb)
        local = lax.rem(cell, cells) + 1
        parts = []
        for k in range(CAPB):
            pick = jnp.logical_and(owned, lax.rem(lane_c, CAPB) == k)
            which = jnp.sum(jnp.where(pick, local, 0), axis=1, keepdims=True) - 1
            asked = one_hot(cell_iota == which)
            asked = jnp.concatenate([asked, jnp.zeros((LANES - tiles, cells), BF16)], axis=0)
            parts.append(nn(back, asked).astype(BF16))
        requests[s] = jnp.concatenate(parts, axis=0)

    sources, slots = chase(me)

    q_iota = lax.broadcasted_iota(jnp.int32, (cols, cols), 0)
    j_iota = lax.broadcasted_iota(jnp.int32, (cols, cols), 1)
    relax = jnp.where(j_iota < nb, 1.0 - RELAX_RATE, 1.0)
    moves = [None] * STEPS
    path = None
    for s in range(STEPS - 1, -1, -1):
        hop = jnp.where(slots[s] == q_iota, relax, 0.0).astype(BF16)
        path = hop if path is None else nn(path, hop).astype(BF16)
        moves[s] = path

    def fill(level, _):
        own = pltpu.roll(held[pl.ds(pl.multiple_of(level * rows, rows), rows), :], half, axis=0)
        top = jnp.where(row_i < half, 0.0, own)
        bottom = jnp.where(row_i < half, own, 0.0)
        w[pl.ds(pl.multiple_of(level * tall, tall), tall), :] = jnp.concatenate([top, bottom], axis=0)
        return 0

    lax.fori_loop(0, tall_mixed, fill, 0, unroll=8)

    slot_rows = STEPS * CAPB

    def pick(s):
        fields = []
        for m in range(members):
            pieces = [
                w[pl.ds(m * levels * tall + half + r, padded, stride=tall), :] for r in range(rows)
            ]
            fields.append(jnp.concatenate(pieces, axis=1))
            fields.append(jnp.zeros((LANES - padded, cells), F32))
        values = nt(requests[s], jnp.concatenate(fields, axis=0).astype(BF16))
        for k in range(CAPB):
            for m in range(members):
                msg[m, pl.ds(s * CAPB + k, tiles, stride=slot_rows), :] = values[
                    k * tiles : (k + 1) * tiles, m * LANES : (m + 1) * LANES
                ]

    pick(0)

    row_t = lax.broadcasted_iota(jnp.int32, (tall, width), 0) + me * rows - half
    inside = jnp.logical_and(row_t >= 0, row_t < tiles * rows)
    for i in range(2):
        @pl.when(has[1 - i])
        def _():
            for copy in halo_pair(i, me):
                copy.wait_recv()
            for d in range(half):
                row = half - 1 - d if i == 0 else half + rows + d
                came = halo_in[i, d * tall_mixed : (d + 1) * tall_mixed, :].astype(F32)
                if d == 0:
                    came = came + halo_in[i, half * tall_mixed :, :].astype(F32)
                w[pl.ds(row, tall_mixed, stride=tall), :] = came

        @pl.when(jnp.logical_not(has[1 - i]))
        def _():
            terr_in[i] = jnp.zeros((rows, width), jnp.int32)

    terr = terrain_ref[...]
    terr_own = pltpu.roll(terr, half, axis=0)
    terr_all = jnp.concatenate(
        [
            jnp.where(row_i < half, pltpu.roll(terr_in[0], half, axis=0), terr_own),
            jnp.where(row_i < half, terr_own, pltpu.roll(terr_in[1], half, axis=0)),
        ],
        axis=0,
    )
    damping = DRAG_RATE * terr_all.astype(F32) / 3000.0
    centre = 1.0 - 4.0 * HORIZ_MIX - 2.0 * VERT_MIX - damping

    chunk = 9 if levels % 9 == 0 else 1

    def advance(final):
        def body(c, before):
            before = list(before)
            for u in range(chunk):
                level = c * chunk + u
                for m in range(members):
                    base = pl.multiple_of((m * levels + level) * tall, tall)
                    above = pl.multiple_of(
                        (m * levels + jnp.minimum(level + 1, levels - 1)) * tall, tall
                    )
                    cur = w[pl.ds(base, tall), :]
                    up = w[pl.ds(above, tall), :]
                    sides = (
                        pltpu.roll(cur, 1, axis=0) + pltpu.roll(cur, tall - 1, axis=0)
                        + pltpu.roll(cur, 1, axis=1) + pltpu.roll(cur, width - 1, axis=1)
                    )
                    new = centre * cur + HORIZ_MIX * sides + VERT_MIX * (up + before[m])
                    if final:
                        parent_out[pl.ds(pl.multiple_of((m * levels + level) * rows, rows), rows), :] = new[half : half + rows]
                    else:
                        w[pl.ds(base, tall), :] = jnp.where(inside, new, 0.0)
                    before[m] = cur
            return tuple(before)

        first = tuple(w[m * levels * tall : (m * levels + 1) * tall, :] for m in range(members))
        lax.fori_loop(0, levels // chunk, body, first)

    advance(False)
    pick(1)

    for d in range(1, zs):
        rcopy(
            zg.at[my_z], zg.at[lax.rem(my_z + zs - d, zs)], z_s.at[d], z_r.at[d], me
        ).wait_recv()

    def masked(origin, m):
        out = jnp.zeros((padded, cols), F32)
        for z in range(zs):
            out = jnp.where(origin == z * PLANE + my_p, zg[z, m], out)
        return out

    for d in range(1, PLANE):
        final = my_z * PLANE + lax.rem(my_p + d, PLANE)
        origin = chase(final)[0][0]
        for m in range(members):
            pm[d - 1, m] = masked(origin, m)
        start(rcopy(pm.at[d - 1], pr.at[d - 1], p_s.at[d], p_r.at[d], final))

    for s in range(2, STEPS):
        advance(False)
        pick(s)

    def rows_of(tile):
        return pl.ds(pl.multiple_of(tile * slot_rows, slot_rows), slot_rows)

    for d in range(1, tiles):
        start(rcopy(msg.at[:, rows_of(at(d))], got.at[:, rows_of(me)], msg_s.at[d], msg_r.at[d], at(d)))
    got[:, rows_of(me), :] = msg[:, rows_of(me), :]

    advance(True)

    origin = sources[0]
    for d in range(1, PLANE):
        rcopy(pm.at[d - 1], pr.at[d - 1], p_s.at[d], p_r.at[d], me).wait_recv()
    result = []
    for m in range(members):
        block = masked(origin, m)
        for d in range(1, PLANE):
            came = lax.rem(origin, PLANE) == lax.rem(my_p + PLANE - d, PLANE)
            block = jnp.where(came, pr[d - 1, m], block)
        result.append(nt(block, moves[0].astype(F32), HI))

    g_rows = tiles * slot_rows
    lane_1 = lax.broadcasted_iota(jnp.int32, (SUB, LANES), 1)
    row_1 = lax.broadcasted_iota(jnp.int32, (SUB, cols), 0)
    lane_j = lax.broadcasted_iota(jnp.int32, (SUB, cols), 1)
    weight = jnp.zeros((SUB, LANES), F32)
    place = jnp.zeros((SUB, LANES), F32)
    for s in range(STEPS):
        asker = sources[s][:, 0:1]
        cell = jnp.sum(
            jnp.where(t_iota == asker, meta[:, STEPS + s, :], 0), axis=0, keepdims=True
        )
        fed = (cell // cells) * slot_rows + s * CAPB + lax.rem(lane_j, CAPB)
        table = jnp.where(row_1 == 0, 1, fed)
        table = jnp.where(lane_j < nb, table, 0).astype(F32).astype(BF16)
        hot = jnp.where(moves[s] > 0, 1.0, 0.0).astype(BF16)
        here = lane_1 // per == s
        moved = pltpu.roll(nt(table, moves[s])[:, :LANES], s * per, axis=1)
        weight = jnp.where(here, moved, weight)
        moved = pltpu.roll(nt(table, hot)[:, :LANES], s * per, axis=1)
        place = jnp.where(here, moved, place)
    place = place[1:2].astype(jnp.int32)
    g_iota = lax.broadcasted_iota(jnp.int32, (g_rows, LANES), 0)
    takes = jnp.where(g_iota == place, weight[0:1], 0.0).astype(BF16)

    for d in range(1, tiles):
        rcopy(
            msg.at[:, rows_of(me)], got.at[:, rows_of(at(tiles - d))], msg_s.at[d], msg_r.at[d], me
        ).wait_recv()
    entries = [nn(jnp.transpose(got[m]).astype(BF16), takes).astype(BF16) for m in range(members)]
    solved = nn(parts_ref[...], jnp.concatenate(entries, axis=1))
    lane_p = lax.broadcasted_iota(jnp.int32, (padded, LANES), 1)
    for m in range(members):
        added = jnp.zeros((padded, LANES), F32)
        for s in range(STEPS):
            terms = [
                solved[(s * PARTS + part) * padded : (s * PARTS + part + 1) * padded,
                       m * LANES : (m + 1) * LANES]
                for part in range(PARTS)
            ]
            added = jnp.where(lane_p // per == s, terms[0] + (terms[1] + terms[2]), added)
        span = LANES // 2
        while span >= per:
            added = added + pltpu.roll(added, span, axis=1)
            span //= 2
        added = jnp.where(lane_p < per, added, 0.0)
        if cols > LANES:
            added = jnp.concatenate([added, jnp.zeros((padded, cols - LANES), F32)], axis=1)
        full = result[m] + added
        mine[m] = full
        nest_out[m] = full[:levels]

    pair = rcopy(mine, theirs, mem_s, mem_r, me, 1 - core)
    pair.start()
    pair.wait()
    count = 2 * members
    fields = [mine[m, 0:levels] for m in range(members)]
    fields += [theirs[m, 0:levels] for m in range(members)]
    mean = functools.reduce(lambda a, b: a + b, fields) / count
    mean_out[...] = mean
    var_out[...] = functools.reduce(lambda a, b: a + b, [(f - mean) ** 2 for f in fields]) / count

    for copy in pending:
        copy.wait_send()
    for i in range(2):
        @pl.when(has[i])
        def _():
            for copy in halo_pair(i, to[i]):
                copy.wait_send()


def on_device_fused(parent_state, nest_state, terrain, shift_x, boundary_index, reloc_dest):
    members, levels, rows, width = parent_state.shape
    cols = nest_state.shape[2]
    nb = boundary_index.shape[1]
    tiles = lax.axis_size("tile")
    cells = rows * width
    padded = -(-levels // 8) * 8
    zs = tiles // PLANE
    slot_rows = STEPS * CAPB
    mixed = members * levels
    tall_mixed = -(-mixed // SUB) * SUB
    dims = (members, levels, rows, width, cols, nb, tiles, cols // (tiles // 2), cells)
    vmem = pl.BlockSpec(memory_space=pltpu.VMEM)
    dma = pltpu.SemaphoreType.DMA
    last, parts = inverse_powers(levels)
    outs = pl.pallas_call(
        functools.partial(fused, dims),
        out_shape=(
            jax.ShapeDtypeStruct((mixed * rows, width), F32),
            jax.ShapeDtypeStruct((members, levels, cols), F32),
            jax.ShapeDtypeStruct((levels, cols), F32),
            jax.ShapeDtypeStruct((levels, cols), F32),
        ),
        in_specs=[pl.BlockSpec(memory_space=pltpu.HBM), vmem, vmem, pl.BlockSpec(memory_space=pltpu.SMEM)] + [vmem] * 4,
        out_specs=(vmem,) * 4,
        scratch_shapes=[
            pltpu.VMEM((tall_mixed * rows, width), F32),
            pltpu.VMEM((tiles, 2 * STEPS, cols), jnp.int32),
            pltpu.VMEM((2, (rows // 2 + 1) * tall_mixed, width), BF16),
            pltpu.VMEM((2, (rows // 2 + 1) * tall_mixed, width), BF16),
            pltpu.VMEM((2, rows, width), jnp.int32),
            pltpu.VMEM((zs, members, padded, cols), F32),
            pltpu.VMEM((PLANE - 1, members, padded, cols), F32),
            pltpu.VMEM((PLANE - 1, members, padded, cols), F32),
            pltpu.VMEM((tall_mixed * 2 * rows, width), F32),
            pltpu.VMEM((members, tiles * slot_rows, LANES), F32),
            pltpu.VMEM((members, tiles * slot_rows, LANES), F32),
            pltpu.VMEM((members, padded, cols), F32),
            pltpu.VMEM((members, padded, cols), F32),
            dma,
            dma((tiles,)), dma((tiles,)),
            dma((2,)), dma((2,)), dma((2,)), dma((2,)),
            dma((zs,)), dma((zs,)), dma((PLANE,)), dma((PLANE,)),
            dma((tiles,)), dma((tiles,)),
            dma, dma,
        ],
        compiler_params=pltpu.CompilerParams(
            collective_id=0, has_side_effects=True, vmem_limit_bytes=63 * 1024 * 1024
        ),
    )(
        parent_state.reshape(mixed * rows, width),
        nest_state, terrain, shift_x, boundary_index, reloc_dest,
        jnp.asarray(last), jnp.asarray(parts),
    )
    return (outs[0].reshape(parent_state.shape),) + tuple(outs[1:])


def fits_one_plane_split(mesh, parent, nest, bound):
    tiles = mesh.shape["tile"]
    cols = nest[2] // tiles
    return (
        tiles == PLANE * PLANE
        and mesh.shape["member"] == 2
        and bound[1] // tiles <= cols // (tiles // 2)
        and nest[1] <= LANES
        and nest[0] == 4
        and parent[2] // tiles == 2 * STEPS
        and parent[3] == LANES
        and cols % LANES == 0
        and STEPS * (cols // (tiles // 2)) == LANES
    )


def solution(mesh):
    in_specs = (
        P("member", None, "tile", None),
        P("member", None, "tile"),
        P("tile", None),
        P(),
        P(None, "tile"),
        P(None, "tile"),
    )
    out_specs = (
        P("member", None, "tile", None),
        P("member", None, "tile"),
        P(None, "tile"),
        P(None, "tile"),
    )

    def whole(parent_state, nest_state, terrain, shift_x, boundary_index, reloc_dest):
        fits = fits_one_plane_split(mesh, parent_state.shape, nest_state.shape, boundary_index.shape)
        return jax.shard_map(
            on_device_fused if fits else on_device,
            mesh=mesh, in_specs=in_specs, out_specs=out_specs, check_vma=False,
        )(parent_state, nest_state, terrain, shift_x, boundary_index, reloc_dest)

    return whole
```

```python
import functools

import jax
import jax.numpy as jnp
import numpy as np
from jax import lax
from jax.experimental import pallas as pl
from jax.experimental.pallas import tpu as pltpu
from jax.sharding import PartitionSpec as P

CAPB = 2
STEPS = 4


HORIZ_MIX = 0.15
VERT_MIX = 0.1
DRAG_RATE = 0.1
RELAX_RATE = 0.5
IMPLICIT_MIX = 0.8


def with_halo(block, sides, width):
    for axis, dim in sides:
        count = lax.axis_size(axis)
        forward = [(i, i + 1) for i in range(count - 1)]
        backward = [(target, source) for source, target in forward]
        low = lax.ppermute(
            lax.slice_in_dim(block, block.shape[dim] - width, None, axis=dim), axis, forward
        )
        high = lax.ppermute(lax.slice_in_dim(block, 0, width, axis=dim), axis, backward)
        block = jnp.concatenate([low, block, high], axis=dim)
    return block


def parent_update(parent, damping):
    padded = with_halo(parent, (("tile", 2),), 1)
    north_row = padded[:, :, 2:, :]
    south_row = padded[:, :, :-2, :]
    east_cell = jnp.roll(parent, -1, axis=3)
    west_cell = jnp.roll(parent, 1, axis=3)
    upper_level = jnp.concatenate([parent[:, 1:], parent[:, -1:]], axis=1)
    lower_level = jnp.concatenate([parent[:, :1], parent[:, :-1]], axis=1)
    return (
        parent
        + HORIZ_MIX * (north_row + south_row + east_cell + west_cell - 4.0 * parent)
        + VERT_MIX * (upper_level + lower_level - 2.0 * parent)
        - damping * parent
    )


def implicit_column(column_field):
    levels = column_field.shape[1]
    pivots = []
    cprime = []
    previous = 0.0
    for level in range(levels):
        neighbours = (1 if level > 0 else 0) + (1 if level < levels - 1 else 0)
        diagonal = 1.0 + IMPLICIT_MIX * neighbours
        pivot = diagonal - IMPLICIT_MIX * previous if level > 0 else diagonal
        previous = IMPLICIT_MIX / pivot
        pivots.append(pivot)
        cprime.append(previous)
    sweep = []
    forward = None
    for level in range(levels):
        source = column_field[:, level]
        if level > 0:
            source = source + IMPLICIT_MIX * forward
        forward = source / pivots[level]
        sweep.append(forward)
    result = [None] * levels
    result[levels - 1] = sweep[levels - 1]
    for level in range(levels - 2, -1, -1):
        result[level] = sweep[level] + cprime[level] * result[level + 1]
    return jnp.stack(result, axis=1)


def locate(indices, shift_by, row_width, tile_cells):
    rows_at = indices // row_width
    cols_at = jnp.mod(indices % row_width + shift_by, row_width)
    moved = rows_at * row_width + cols_at
    return (moved // tile_cells, moved % tile_cells)


def on_device(parent_state, nest_state, terrain, shift_x, boundary_index, reloc_dest):
    members, levels, rows_here, row_width = parent_state.shape
    columns_here = nest_state.shape[2]
    tile_count = lax.axis_size("tile")
    tile_cells = rows_here * row_width
    boundary_here = boundary_index.shape[1]
    owners = boundary_here // CAPB
    mixed = members * levels
    groups = tile_count // 2
    per_peer = columns_here // groups
    damping = DRAG_RATE * terrain.astype(jnp.float32) / 3000.0
    parent = parent_state
    nest_field = nest_state
    for step_no in range(STEPS):
        flat_parent = parent.astype(jnp.bfloat16).reshape(mixed, tile_cells)
        offset = shift_x[step_no]
        owner_of, local_of = locate(boundary_index[step_no], offset, row_width, tile_cells)
        owner_runs = owner_of.reshape(owners, CAPB)[:, 0]
        local_runs = local_of.reshape(owners, CAPB)
        requests_out = jnp.zeros((tile_count, CAPB), jnp.int32).at[owner_runs].set(local_runs)
        values = jnp.transpose(
            jnp.take(
                flat_parent,
                lax.all_to_all(requests_out, "tile", split_axis=0, concat_axis=0, tiled=True),
                axis=1,
            ),
            (1, 2, 0),
        )
        received = lax.all_to_all(values, "tile", split_axis=0, concat_axis=0, tiled=True)
        edge_values = received[owner_runs].reshape(boundary_here, mixed)
        edge_values = (
            jnp.transpose(edge_values).astype(jnp.float32).reshape(members, levels, boundary_here)
        )
        edge_cols = nest_field[:, :, :boundary_here]
        edge_cols = edge_cols + RELAX_RATE * (edge_values - edge_cols)
        nest_field = jnp.concatenate([edge_cols, nest_field[:, :, boundary_here:]], axis=2)
        nest_field = implicit_column(nest_field)
        targets = reloc_dest[step_no].reshape(groups, per_peer)
        target_tile = targets[:, 0] // columns_here
        slots = targets % columns_here
        values_out = jnp.transpose(nest_field.reshape(mixed, groups, per_peer), (1, 2, 0))
        send_values = (
            jnp.zeros((tile_count, per_peer, mixed), jnp.float32).at[target_tile].set(values_out)
        )
        send_slots = (
            jnp.full((tile_count, per_peer), columns_here, jnp.int32).at[target_tile].set(slots)
        )
        got_values, got_slots = (
            lax.all_to_all(send_values, "tile", split_axis=0, concat_axis=0, tiled=True),
            lax.all_to_all(send_slots, "tile", split_axis=0, concat_axis=0, tiled=True),
        )
        placed = (
            jnp.zeros((columns_here, mixed), jnp.float32)
            .at[got_slots.reshape(-1)]
            .set(got_values.reshape(-1, mixed), mode="drop")
        )
        nest_field = jnp.transpose(placed).reshape(members, levels, columns_here)
        parent = parent_update(parent, damping)
    ensemble = members * lax.axis_size("member")
    totals = lax.psum(jnp.sum(nest_field, axis=0), "member")
    mean_field = totals / ensemble
    spread_sum = lax.psum(jnp.sum((nest_field - mean_field) ** 2, axis=0), "member")
    variance = spread_sum / ensemble
    return (parent, nest_field, mean_field, variance)


MESH = pl.DeviceIdType.MESH
F32 = jnp.float32
BF16 = jnp.bfloat16
HI = lax.Precision.HIGHEST
PLANE = 4
LANES = 128
PARTS = 3
SUB = 16
EDGE = 8


def inverse_powers(levels):
    a = np.zeros((levels, levels))
    for level in range(levels):
        a[level, level] = 1.0
        for other in (level - 1, level + 1):
            if 0 <= other < levels:
                a[level, level] += IMPLICIT_MIX
                a[level, other] = -IMPLICIT_MIX
    inv = np.linalg.inv(a)
    padded = -(-levels // 8) * 8
    parts = np.zeros((STEPS, PARTS, padded, LANES), jnp.bfloat16)
    power = np.eye(levels)
    for k in range(STEPS):
        power = power @ inv
        rest = power
        for part in range(PARTS):
            piece = rest.astype(np.float32).astype(jnp.bfloat16)
            parts[STEPS - 1 - k, part, :levels, :levels] = piece
            rest = rest - piece.astype(np.float64)
    last = np.zeros((padded, levels), np.float32)
    last[:levels] = power
    return last, parts.reshape(STEPS * PARTS * padded, LANES)


def nn(a, b, precision=None):
    return lax.dot_general(
        a, b, (((1,), (0,)), ((), ())), preferred_element_type=F32, precision=precision
    )


def nt(a, b, precision=None):
    return lax.dot_general(
        a, b, (((1,), (1,)), ((), ())), preferred_element_type=F32, precision=precision
    )


def one_hot(mask):
    return jnp.where(mask, 1.0, 0.0).astype(BF16)


def fused(
    dims,
    parent_ref, nest_ref, terrain_ref, shift_ref, bound_ref, dest_ref, last_ref, parts_ref,
    parent_out, nest_out, mean_out, var_out,
    meta, halo_out, halo_in, terr_in, zg, pm, pr, w, msg, got, mine, theirs,
    meta_s, meta_r, halo_s, halo_r, terr_s, terr_r, z_s, z_r, p_s, p_r, msg_s, msg_r, mem_s, mem_r,
):
    members, levels, rows, width, cols, nb, tiles, per, cells = dims
    padded = zg.shape[2]
    zs = tiles // PLANE
    tall = 2 * rows
    half = rows // 2
    me = lax.axis_index("tile")
    core = lax.axis_index("member")
    both = members * padded
    my_p = lax.rem(me, PLANE)
    my_z = me // PLANE

    def rcopy(src, dst, ssem, rsem, tile, member=None):
        return pltpu.make_async_remote_copy(
            src_ref=src, dst_ref=dst, send_sem=ssem, recv_sem=rsem,
            device_id=(core if member is None else member, tile), device_id_type=MESH,
        )

    def at(d):
        return lax.rem(me + d, tiles)

    barrier = pltpu.get_barrier_semaphore()
    for d in range(1, tiles):
        pl.semaphore_signal(barrier, inc=1, device_id=(core, at(d)), device_id_type=MESH)
    pl.semaphore_signal(barrier, inc=1, device_id=(1 - core, me), device_id_type=MESH)

    meta[me, 0:STEPS, :] = dest_ref[...]
    meta[me, STEPS : 2 * STEPS, :] = jnp.zeros((STEPS, cols), jnp.int32)
    for s in range(STEPS):
        index = bound_ref[s : s + 1, :]
        at_col = lax.rem(lax.rem(index, width) + shift_ref[s] + width, width)
        meta[me, STEPS + s : STEPS + s + 1, 0:nb] = (index // width) * width + at_col

    for m in range(members):
        zg[my_z, m] = nn(last_ref[...], nest_ref[:, m, :], HI)

    tail = jnp.zeros((w.shape[3] - EDGE - padded + EDGE, width), F32)
    for t in range(STEPS):
        for r in range(tall):
            for m in range(members):
                w[t, r, m, padded:, :] = tail
    for r in range(rows):
        for m in range(members):
            w[0, half + r, m, EDGE : EDGE + levels, :] = parent_ref[
                pl.ds(m * levels * rows + r, levels, stride=rows), :
            ]
    for i in range(2):
        for d in range(half):
            row = half + (rows - 1 - d if i == 0 else d)
            field = jnp.concatenate(
                [w[0, row, m, EDGE : EDGE + padded, :] for m in range(members)], axis=0
            )
            near = field.astype(BF16)
            halo_out[i, d * both : (d + 1) * both, :] = near
            if d == 0:
                halo_out[i, half * both :, :] = (field - near.astype(F32)).astype(BF16)

    pl.semaphore_wait(barrier, tiles)

    pending = []

    def start(copy):
        copy.start()
        pending.append(copy)

    for d in range(1, tiles):
        start(rcopy(meta.at[me], meta.at[me], meta_s.at[d], meta_r.at[d], at(d)))

    def halo_pair(i, tile):
        return (
            rcopy(halo_out.at[i], halo_in.at[i], halo_s.at[i], halo_r.at[i], tile),
            rcopy(terrain_ref, terr_in.at[i], terr_s.at[i], terr_r.at[i], tile),
        )

    has = (me < tiles - 1, me > 0)
    to = (lax.rem(me + 1, tiles), lax.rem(me + tiles - 1, tiles))
    for i in range(2):
        @pl.when(has[i])
        def _():
            for copy in halo_pair(i, to[i]):
                copy.start()

    for d in range(1, zs):
        start(rcopy(zg.at[my_z], zg.at[my_z], z_s.at[d], z_r.at[d], at(d * PLANE)))

    for d in range(1, tiles):
        rcopy(meta.at[me], meta.at[at(tiles - d)], meta_s.at[d], meta_r.at[d], me).wait_recv()

    t_iota = lax.broadcasted_iota(jnp.int32, (tiles, cols), 0)
    dest = [meta[:, s, :] for s in range(STEPS)]
    dest_tile = [v // cols for v in dest]

    def chase(final):
        tau = jnp.zeros((1, cols), jnp.int32) + final
        sources, slots, firsts = [None] * STEPS, [None] * STEPS, [None] * STEPS
        for s in range(STEPS - 1, -1, -1):
            hit = dest_tile[s] == tau
            tau = jnp.sum(jnp.where(hit, t_iota, 0), axis=0, keepdims=True)
            slots[s] = jnp.sum(jnp.where(hit, dest[s] - dest_tile[s] * cols, 0), axis=0, keepdims=True)
            sources[s] = tau
        return sources, slots

    lane_t = lax.broadcasted_iota(jnp.int32, (tiles, LANES), 1)
    lane_c = lax.broadcasted_iota(jnp.int32, (tiles, cols), 1)
    slot_rows = STEPS * CAPB
    wanted = jnp.zeros((1, LANES), jnp.int32)
    path = None
    for s in range(STEPS - 1, -1, -1):
        hop = one_hot(dest_tile[s][:, 0:1] == lane_t // slot_rows)
        if path is None:
            path = hop
        else:
            step_hop = one_hot(dest_tile[s][:, 0:1] == lane_t)
            above = jnp.concatenate([path, jnp.zeros((LANES - tiles, LANES), BF16)], axis=0)
            path = nn(step_hop, above).astype(BF16)
        cell = meta[:, STEPS + s, :]
        owned = jnp.logical_and(cell // cells == me, lane_c < nb)
        local = lax.rem(cell, cells) + 1
        for k in range(CAPB):
            pick_k = jnp.logical_and(owned, lax.rem(lane_c, CAPB) == k)
            which = jnp.sum(jnp.where(pick_k, local, 0), axis=1, keepdims=True)
            there = jnp.logical_and(path > 0, lax.rem(lane_t, slot_rows) == s * CAPB + k)
            wanted = wanted + jnp.sum(jnp.where(there, which, 0), axis=0, keepdims=True)
    cell_iota = lax.broadcasted_iota(jnp.int32, (cells, LANES), 0)
    requests = one_hot(cell_iota == wanted - 1)

    sources, slots = chase(me)

    q_iota = lax.broadcasted_iota(jnp.int32, (cols, cols), 0)
    j_iota = lax.broadcasted_iota(jnp.int32, (cols, cols), 1)
    relax = jnp.where(j_iota < nb, 1.0 - RELAX_RATE, 1.0)
    moves = [None] * STEPS
    path = None
    for s in range(STEPS - 1, -1, -1):
        hop = jnp.where(slots[s] == q_iota, relax, 0.0).astype(BF16)
        path = hop if path is None else nn(path, hop).astype(BF16)
        moves[s] = path

    lane_s = lax.rem(lax.broadcasted_iota(jnp.int32, (both, LANES), 1), slot_rows) // CAPB
    picked = [jnp.zeros((both, LANES), F32)]

    def pick(t):
        field = jnp.concatenate(
            [
                jnp.concatenate(
                    [w[t, half + r, m, EDGE : EDGE + padded, :] for m in range(members)], axis=0
                ).astype(BF16)
                for r in range(rows)
            ],
            axis=1,
        )
        picked[0] = jnp.where(lane_s == t, nn(field, requests), picked[0])

    pick(0)

    def coefficient(terr_row):
        return 1.0 - 4.0 * HORIZ_MIX - 2.0 * VERT_MIX - DRAG_RATE * terr_row.astype(F32) / 3000.0

    def centre_of(r):
        if r < half:
            return coefficient(terr_in[0, rows - half + r : rows - half + r + 1, :])
        if r < half + rows:
            return coefficient(terrain_ref[r - half : r - half + 1, :])
        return coefficient(terr_in[1, r - half - rows : r - half - rows + 1, :])

    def guard(t, r):
        for m in range(members):
            w[t, r, m, EDGE - 1 : EDGE, :] = w[t, r, m, EDGE : EDGE + 1, :]
            w[t, r, m, EDGE + levels : EDGE + levels + 1, :] = w[
                t, r, m, EDGE + levels - 1 : EDGE + levels, :
            ]

    def advance(t, r):
        centre = centre_of(r)
        beyond = None
        if r < half:
            beyond = jnp.where(has[1], 1.0, 0.0)
        elif r >= half + rows:
            beyond = jnp.where(has[0], 1.0, 0.0)
        guard(t, r)
        for m in range(members):
            cur = w[t, r, m, EDGE : EDGE + padded, :]
            up = w[t, r, m, EDGE + 1 : EDGE + 1 + padded, :]
            down = w[t, r, m, EDGE - 1 : EDGE - 1 + padded, :]
            north = w[t, r + 1, m, EDGE : EDGE + padded, :]
            south = w[t, r - 1, m, EDGE : EDGE + padded, :]
            sides = (north + south) + (pltpu.roll(cur, 1, axis=1) + pltpu.roll(cur, width - 1, axis=1))
            new = centre * cur + HORIZ_MIX * sides + VERT_MIX * (up + down)
            if beyond is not None:
                new = new * beyond
            if t == STEPS - 1:
                parent_out[pl.ds(m * levels * rows + r - half, levels, stride=rows), :] = new[:levels]
            else:
                w[t + 1, r, m, EDGE : EDGE + padded, :] = new

    for t in range(STEPS - 1):
        for r in range(half + t + 1, half + rows - t - 1):
            advance(t, r)

    def outer(t):
        inner = range(half + t + 1, half + rows - t - 1)
        for r in range(t + 1, tall - t - 1):
            if r not in inner:
                advance(t, r)

    for i in range(2):
        @pl.when(has[1 - i])
        def _():
            for copy in halo_pair(i, me):
                copy.wait_recv()
            for d in range(half):
                row = half - 1 - d if i == 0 else half + rows + d
                came = halo_in[i, d * both : (d + 1) * both, :].astype(F32)
                if d == 0:
                    came = came + halo_in[i, half * both :, :].astype(F32)
                for m in range(members):
                    w[0, row, m, EDGE : EDGE + padded, :] = came[m * padded : (m + 1) * padded]

        @pl.when(jnp.logical_not(has[1 - i]))
        def _():
            terr_in[i] = jnp.zeros((rows, width), jnp.int32)
            for d in range(half):
                row = half - 1 - d if i == 0 else half + rows + d
                for m in range(members):
                    w[0, row, m, EDGE : EDGE + padded, :] = jnp.zeros((padded, width), F32)

    outer(0)
    pick(1)

    for d in range(1, zs):
        rcopy(
            zg.at[my_z], zg.at[lax.rem(my_z + zs - d, zs)], z_s.at[d], z_r.at[d], me
        ).wait_recv()

    def masked(origin, m):
        out = jnp.zeros((padded, cols), F32)
        for z in range(zs):
            out = jnp.where(origin == z * PLANE + my_p, zg[z, m], out)
        return out

    for d in range(1, PLANE):
        final = my_z * PLANE + lax.rem(my_p + d, PLANE)
        origin = chase(final)[0][0]
        for m in range(members):
            pm[d - 1, m] = masked(origin, m)
        start(rcopy(pm.at[d - 1], pr.at[d - 1], p_s.at[d], p_r.at[d], final))

    for t in range(2, STEPS):
        outer(t - 1)
        pick(t)
    for m in range(members):
        part = picked[0][m * padded : (m + 1) * padded]
        part = jnp.concatenate([part, jnp.zeros((LANES - padded, LANES), F32)], axis=0)
        msg[m] = jnp.transpose(part)

    def rows_of(tile):
        return pl.ds(pl.multiple_of(tile * slot_rows, slot_rows), slot_rows)

    for d in range(1, tiles):
        start(rcopy(msg.at[:, rows_of(at(d))], got.at[:, rows_of(me)], msg_s.at[d], msg_r.at[d], at(d)))
    got[:, rows_of(me), :] = msg[:, rows_of(me), :]

    for r in range(half, half + rows):
        advance(STEPS - 1, r)

    origin = sources[0]
    for d in range(1, PLANE):
        rcopy(pm.at[d - 1], pr.at[d - 1], p_s.at[d], p_r.at[d], me).wait_recv()
    result = []
    for m in range(members):
        block = masked(origin, m)
        for d in range(1, PLANE):
            came = lax.rem(origin, PLANE) == lax.rem(my_p + PLANE - d, PLANE)
            block = jnp.where(came, pr[d - 1, m], block)
        result.append(nt(block, moves[0].astype(F32), HI))

    g_rows = tiles * slot_rows
    lane_1 = lax.broadcasted_iota(jnp.int32, (SUB, LANES), 1)
    row_1 = lax.broadcasted_iota(jnp.int32, (SUB, cols), 0)
    lane_j = lax.broadcasted_iota(jnp.int32, (SUB, cols), 1)
    weight = jnp.zeros((SUB, LANES), F32)
    place = jnp.zeros((SUB, LANES), F32)
    for s in range(STEPS):
        asker = sources[s][:, 0:1]
        cell = jnp.sum(
            jnp.where(t_iota == asker, meta[:, STEPS + s, :], 0), axis=0, keepdims=True
        )
        fed = (cell // cells) * slot_rows + s * CAPB + lax.rem(lane_j, CAPB)
        table = jnp.where(row_1 == 0, 1, fed)
        table = jnp.where(lane_j < nb, table, 0).astype(F32).astype(BF16)
        hot = jnp.where(moves[s] > 0, 1.0, 0.0).astype(BF16)
        here = lane_1 // per == s
        moved = pltpu.roll(nt(table, moves[s])[:, :LANES], s * per, axis=1)
        weight = jnp.where(here, moved, weight)
        moved = pltpu.roll(nt(table, hot)[:, :LANES], s * per, axis=1)
        place = jnp.where(here, moved, place)
    place = place[1:2].astype(jnp.int32)
    g_iota = lax.broadcasted_iota(jnp.int32, (g_rows, LANES), 0)
    takes = jnp.where(g_iota == place, weight[0:1], 0.0).astype(BF16)

    for d in range(1, tiles):
        rcopy(
            msg.at[:, rows_of(me)], got.at[:, rows_of(at(tiles - d))], msg_s.at[d], msg_r.at[d], me
        ).wait_recv()
    entries = [nn(jnp.transpose(got[m]).astype(BF16), takes).astype(BF16) for m in range(members)]
    solved = nn(parts_ref[...], jnp.concatenate(entries, axis=1))
    lane_p = lax.broadcasted_iota(jnp.int32, (padded, LANES), 1)
    for m in range(members):
        added = jnp.zeros((padded, LANES), F32)
        for s in range(STEPS):
            terms = [
                solved[(s * PARTS + part) * padded : (s * PARTS + part + 1) * padded,
                       m * LANES : (m + 1) * LANES]
                for part in range(PARTS)
            ]
            added = jnp.where(lane_p // per == s, terms[0] + (terms[1] + terms[2]), added)
        span = LANES // 2
        while span >= per:
            added = added + pltpu.roll(added, span, axis=1)
            span //= 2
        added = jnp.where(lane_p < per, added, 0.0)
        if cols > LANES:
            added = jnp.concatenate([added, jnp.zeros((padded, cols - LANES), F32)], axis=1)
        full = result[m] + added
        mine[m] = full
        nest_out[m] = full[:levels]

    pair = rcopy(mine, theirs, mem_s, mem_r, me, 1 - core)
    pair.start()
    pair.wait()
    count = 2 * members
    fields = [mine[m, 0:levels] for m in range(members)]
    fields += [theirs[m, 0:levels] for m in range(members)]
    mean = functools.reduce(lambda a, b: a + b, fields) / count
    mean_out[...] = mean
    var_out[...] = functools.reduce(lambda a, b: a + b, [(f - mean) ** 2 for f in fields]) / count

    for copy in pending:
        copy.wait_send()
    for i in range(2):
        @pl.when(has[i])
        def _():
            for copy in halo_pair(i, to[i]):
                copy.wait_send()


def write_out(parent_ref, nest_ref, mean_ref, var_ref, parent_out, nest_out, mean_out, var_out, sems):
    copies = [
        pltpu.make_async_copy(parent_ref, parent_out, sems.at[0]),
        pltpu.make_async_copy(mean_ref, mean_out, sems.at[1]),
        pltpu.make_async_copy(var_ref, var_out, sems.at[2]),
    ]
    for copy in copies:
        copy.start()
    for m in range(nest_ref.shape[0]):
        nest_out[:, m, :] = nest_ref[m]
    for copy in copies:
        copy.wait()


def on_device_fused(parent_state, nest_state, terrain, shift_x, boundary_index, reloc_dest):
    members, levels, rows, width = parent_state.shape
    cols = nest_state.shape[2]
    nb = boundary_index.shape[1]
    tiles = lax.axis_size("tile")
    cells = rows * width
    padded = -(-levels // 8) * 8
    zs = tiles // PLANE
    slot_rows = STEPS * CAPB
    mixed = members * levels
    both = members * padded
    dims = (members, levels, rows, width, cols, nb, tiles, cols // (tiles // 2), cells)
    vmem = pl.BlockSpec(memory_space=pltpu.VMEM)
    dma = pltpu.SemaphoreType.DMA
    last, parts = inverse_powers(levels)
    outs = pl.pallas_call(
        functools.partial(fused, dims),
        out_shape=(
            jax.ShapeDtypeStruct((mixed * rows, width), F32),
            jax.ShapeDtypeStruct((members, levels, cols), F32),
            jax.ShapeDtypeStruct((levels, cols), F32),
            jax.ShapeDtypeStruct((levels, cols), F32),
        ),
        in_specs=[vmem, vmem, vmem, pl.BlockSpec(memory_space=pltpu.SMEM)] + [vmem] * 4,
        out_specs=(vmem,) * 4,
        scratch_shapes=[
            pltpu.VMEM((tiles, 2 * STEPS, cols), jnp.int32),
            pltpu.VMEM((2, (rows // 2 + 1) * both, width), BF16),
            pltpu.VMEM((2, (rows // 2 + 1) * both, width), BF16),
            pltpu.VMEM((2, rows, width), jnp.int32),
            pltpu.VMEM((zs, members, padded, cols), F32),
            pltpu.VMEM((PLANE - 1, members, padded, cols), F32),
            pltpu.VMEM((PLANE - 1, members, padded, cols), F32),
            pltpu.VMEM((STEPS, 2 * rows, members, padded + 2 * EDGE, width), F32),
            pltpu.VMEM((members, tiles * slot_rows, LANES), F32),
            pltpu.VMEM((members, tiles * slot_rows, LANES), F32),
            pltpu.VMEM((members, padded, cols), F32),
            pltpu.VMEM((members, padded, cols), F32),
            dma((tiles,)), dma((tiles,)),
            dma((2,)), dma((2,)), dma((2,)), dma((2,)),
            dma((zs,)), dma((zs,)), dma((PLANE,)), dma((PLANE,)),
            dma((tiles,)), dma((tiles,)),
            dma, dma,
        ],
        compiler_params=pltpu.CompilerParams(
            collective_id=0, has_side_effects=True, vmem_limit_bytes=32 * 1024 * 1024
        ),
    )(
        parent_state.reshape(mixed * rows, width),
        jnp.transpose(nest_state, (1, 0, 2)), terrain, shift_x, boundary_index, reloc_dest,
        jnp.asarray(last), jnp.asarray(parts),
    )
    hbm = pl.BlockSpec(memory_space=pl.ANY)
    outs = pl.pallas_call(
        write_out,
        out_shape=(
            jax.ShapeDtypeStruct((mixed * rows, width), F32),
            jax.ShapeDtypeStruct((levels, members, cols), F32),
            jax.ShapeDtypeStruct((levels, cols), F32),
            jax.ShapeDtypeStruct((levels, cols), F32),
        ),
        in_specs=[vmem] * 4,
        out_specs=(hbm, vmem, hbm, hbm),
        scratch_shapes=[dma((3,))],
        compiler_params=pltpu.CompilerParams(vmem_limit_bytes=16 * 1024 * 1024),
    )(*outs)
    nest_field = jnp.transpose(outs[1], (1, 0, 2))
    return (outs[0].reshape(parent_state.shape), nest_field, outs[2], outs[3])


def fits_one_plane_split(mesh, parent, nest, bound):
    tiles = mesh.shape["tile"]
    cols = nest[2] // tiles
    return (
        tiles == PLANE * PLANE
        and mesh.shape["member"] == 2
        and bound[1] // tiles <= cols // (tiles // 2)
        and nest[1] <= LANES
        and nest[0] == 4
        and parent[2] // tiles == 2 * STEPS
        and parent[3] == LANES
        and cols % LANES == 0
        and STEPS * (cols // (tiles // 2)) == LANES
    )


def solution(mesh):
    in_specs = (
        P("member", None, "tile", None),
        P("member", None, "tile"),
        P("tile", None),
        P(),
        P(None, "tile"),
        P(None, "tile"),
    )
    out_specs = (
        P("member", None, "tile", None),
        P("member", None, "tile"),
        P(None, "tile"),
        P(None, "tile"),
    )

    def whole(parent_state, nest_state, terrain, shift_x, boundary_index, reloc_dest):
        fits = fits_one_plane_split(mesh, parent_state.shape, nest_state.shape, boundary_index.shape)
        return jax.shard_map(
            on_device_fused if fits else on_device,
            mesh=mesh, in_specs=in_specs, out_specs=out_specs, check_vma=False,
        )(parent_state, nest_state, terrain, shift_x, boundary_index, reloc_dest)

    return whole
```

```python
import functools

import jax
import jax.numpy as jnp
import numpy as np
from jax import lax
from jax.experimental import pallas as pl
from jax.experimental.pallas import tpu as pltpu
from jax.sharding import PartitionSpec as P

CAPB = 2
STEPS = 4


HORIZ_MIX = 0.15
VERT_MIX = 0.1
DRAG_RATE = 0.1
RELAX_RATE = 0.5
IMPLICIT_MIX = 0.8


def with_halo(block, sides, width):
    for axis, dim in sides:
        count = lax.axis_size(axis)
        forward = [(i, i + 1) for i in range(count - 1)]
        backward = [(target, source) for source, target in forward]
        low = lax.ppermute(
            lax.slice_in_dim(block, block.shape[dim] - width, None, axis=dim), axis, forward
        )
        high = lax.ppermute(lax.slice_in_dim(block, 0, width, axis=dim), axis, backward)
        block = jnp.concatenate([low, block, high], axis=dim)
    return block


def parent_update(parent, damping):
    padded = with_halo(parent, (("tile", 2),), 1)
    north_row = padded[:, :, 2:, :]
    south_row = padded[:, :, :-2, :]
    east_cell = jnp.roll(parent, -1, axis=3)
    west_cell = jnp.roll(parent, 1, axis=3)
    upper_level = jnp.concatenate([parent[:, 1:], parent[:, -1:]], axis=1)
    lower_level = jnp.concatenate([parent[:, :1], parent[:, :-1]], axis=1)
    return (
        parent
        + HORIZ_MIX * (north_row + south_row + east_cell + west_cell - 4.0 * parent)
        + VERT_MIX * (upper_level + lower_level - 2.0 * parent)
        - damping * parent
    )


def implicit_column(column_field):
    levels = column_field.shape[1]
    pivots = []
    cprime = []
    previous = 0.0
    for level in range(levels):
        neighbours = (1 if level > 0 else 0) + (1 if level < levels - 1 else 0)
        diagonal = 1.0 + IMPLICIT_MIX * neighbours
        pivot = diagonal - IMPLICIT_MIX * previous if level > 0 else diagonal
        previous = IMPLICIT_MIX / pivot
        pivots.append(pivot)
        cprime.append(previous)
    sweep = []
    forward = None
    for level in range(levels):
        source = column_field[:, level]
        if level > 0:
            source = source + IMPLICIT_MIX * forward
        forward = source / pivots[level]
        sweep.append(forward)
    result = [None] * levels
    result[levels - 1] = sweep[levels - 1]
    for level in range(levels - 2, -1, -1):
        result[level] = sweep[level] + cprime[level] * result[level + 1]
    return jnp.stack(result, axis=1)


def locate(indices, shift_by, row_width, tile_cells):
    rows_at = indices // row_width
    cols_at = jnp.mod(indices % row_width + shift_by, row_width)
    moved = rows_at * row_width + cols_at
    return (moved // tile_cells, moved % tile_cells)


def on_device(parent_state, nest_state, terrain, shift_x, boundary_index, reloc_dest):
    members, levels, rows_here, row_width = parent_state.shape
    columns_here = nest_state.shape[2]
    tile_count = lax.axis_size("tile")
    tile_cells = rows_here * row_width
    boundary_here = boundary_index.shape[1]
    owners = boundary_here // CAPB
    mixed = members * levels
    groups = tile_count // 2
    per_peer = columns_here // groups
    damping = DRAG_RATE * terrain.astype(jnp.float32) / 3000.0
    parent = parent_state
    nest_field = nest_state
    for step_no in range(STEPS):
        flat_parent = parent.astype(jnp.bfloat16).reshape(mixed, tile_cells)
        offset = shift_x[step_no]
        owner_of, local_of = locate(boundary_index[step_no], offset, row_width, tile_cells)
        owner_runs = owner_of.reshape(owners, CAPB)[:, 0]
        local_runs = local_of.reshape(owners, CAPB)
        requests_out = jnp.zeros((tile_count, CAPB), jnp.int32).at[owner_runs].set(local_runs)
        values = jnp.transpose(
            jnp.take(
                flat_parent,
                lax.all_to_all(requests_out, "tile", split_axis=0, concat_axis=0, tiled=True),
                axis=1,
            ),
            (1, 2, 0),
        )
        received = lax.all_to_all(values, "tile", split_axis=0, concat_axis=0, tiled=True)
        edge_values = received[owner_runs].reshape(boundary_here, mixed)
        edge_values = (
            jnp.transpose(edge_values).astype(jnp.float32).reshape(members, levels, boundary_here)
        )
        edge_cols = nest_field[:, :, :boundary_here]
        edge_cols = edge_cols + RELAX_RATE * (edge_values - edge_cols)
        nest_field = jnp.concatenate([edge_cols, nest_field[:, :, boundary_here:]], axis=2)
        nest_field = implicit_column(nest_field)
        targets = reloc_dest[step_no].reshape(groups, per_peer)
        target_tile = targets[:, 0] // columns_here
        slots = targets % columns_here
        values_out = jnp.transpose(nest_field.reshape(mixed, groups, per_peer), (1, 2, 0))
        send_values = (
            jnp.zeros((tile_count, per_peer, mixed), jnp.float32).at[target_tile].set(values_out)
        )
        send_slots = (
            jnp.full((tile_count, per_peer), columns_here, jnp.int32).at[target_tile].set(slots)
        )
        got_values, got_slots = (
            lax.all_to_all(send_values, "tile", split_axis=0, concat_axis=0, tiled=True),
            lax.all_to_all(send_slots, "tile", split_axis=0, concat_axis=0, tiled=True),
        )
        placed = (
            jnp.zeros((columns_here, mixed), jnp.float32)
            .at[got_slots.reshape(-1)]
            .set(got_values.reshape(-1, mixed), mode="drop")
        )
        nest_field = jnp.transpose(placed).reshape(members, levels, columns_here)
        parent = parent_update(parent, damping)
    ensemble = members * lax.axis_size("member")
    totals = lax.psum(jnp.sum(nest_field, axis=0), "member")
    mean_field = totals / ensemble
    spread_sum = lax.psum(jnp.sum((nest_field - mean_field) ** 2, axis=0), "member")
    variance = spread_sum / ensemble
    return (parent, nest_field, mean_field, variance)


MESH = pl.DeviceIdType.MESH
F32 = jnp.float32
BF16 = jnp.bfloat16
HI = lax.Precision.HIGHEST
PLANE = 4
LANES = 128
PARTS = 3
SUB = 16
EDGE = 8
WRITES = 2


def inverse_powers(levels):
    a = np.zeros((levels, levels))
    for level in range(levels):
        a[level, level] = 1.0
        for other in (level - 1, level + 1):
            if 0 <= other < levels:
                a[level, level] += IMPLICIT_MIX
                a[level, other] = -IMPLICIT_MIX
    inv = np.linalg.inv(a)
    padded = -(-levels // 8) * 8
    parts = np.zeros((STEPS, PARTS, padded, LANES), jnp.bfloat16)
    power = np.eye(levels)
    for k in range(STEPS):
        power = power @ inv
        rest = power
        for part in range(PARTS):
            piece = rest.astype(np.float32).astype(jnp.bfloat16)
            parts[STEPS - 1 - k, part, :levels, :levels] = piece
            rest = rest - piece.astype(np.float64)
    last = np.zeros((padded, levels), np.float32)
    last[:levels] = power
    return last, parts.reshape(STEPS * PARTS * padded, LANES)


def nn(a, b, precision=None):
    return lax.dot_general(
        a, b, (((1,), (0,)), ((), ())), preferred_element_type=F32, precision=precision
    )


def nt(a, b, precision=None):
    return lax.dot_general(
        a, b, (((1,), (1,)), ((), ())), preferred_element_type=F32, precision=precision
    )


def one_hot(mask):
    return jnp.where(mask, 1.0, 0.0).astype(BF16)


def fused(
    dims,
    parent_in, nest_in, terrain_in, shift_ref, bound_in, dest_in, last_in, parts_in,
    parent_hbm, nest_out, mean_out, var_out,
    parent_ref, nest_ref, terrain_ref, bound_ref, dest_ref, last_ref, parts_ref, in_s,
    parent_out, out_s,
    meta, halo_out, halo_in, terr_in, zg, pm, pr, w, msg, got, mine, theirs,
    meta_s, meta_r, halo_s, halo_r, terr_s, terr_r, z_s, z_r, p_s, p_r, msg_s, msg_r, mem_s, mem_r,
):
    members, levels, rows, width, cols, nb, tiles, per, cells = dims
    padded = zg.shape[2]
    zs = tiles // PLANE
    tall = 2 * rows
    half = rows // 2
    me = lax.axis_index("tile")
    core = lax.axis_index("member")
    both = members * padded
    my_p = lax.rem(me, PLANE)
    my_z = me // PLANE

    def rcopy(src, dst, ssem, rsem, tile, member=None):
        return pltpu.make_async_remote_copy(
            src_ref=src, dst_ref=dst, send_sem=ssem, recv_sem=rsem,
            device_id=(core if member is None else member, tile), device_id_type=MESH,
        )

    def at(d):
        return lax.rem(me + d, tiles)

    barrier = pltpu.get_barrier_semaphore()
    for d in range(1, tiles):
        pl.semaphore_signal(barrier, inc=1, device_id=(core, at(d)), device_id_type=MESH)
    pl.semaphore_signal(barrier, inc=1, device_id=(1 - core, me), device_id_type=MESH)

    sources_in = (parent_in, dest_in, bound_in, terrain_in, nest_in, last_in, parts_in)
    places_in = (parent_ref, dest_ref, bound_ref, terrain_ref, nest_ref, last_ref, parts_ref)
    fetches = [
        pltpu.make_async_copy(a, b, in_s.at[i])
        for i, (a, b) in enumerate(zip(sources_in, places_in))
    ]
    for fetch in fetches:
        fetch.start()

    tail = jnp.zeros((w.shape[3] - EDGE - padded + EDGE, width), F32)
    for t in range(STEPS):
        for r in range(tall):
            for m in range(members):
                w[t, r, m, padded:, :] = tail
    fetches[0].wait()
    for r in range(rows):
        for m in range(members):
            w[0, half + r, m, EDGE : EDGE + levels, :] = parent_ref[
                pl.ds(m * levels * rows + r, levels, stride=rows), :
            ]
    for i in range(2):
        for d in range(half):
            row = half + (rows - 1 - d if i == 0 else d)
            field = jnp.concatenate(
                [w[0, row, m, EDGE : EDGE + padded, :] for m in range(members)], axis=0
            )
            near = field.astype(BF16)
            halo_out[i, d * both : (d + 1) * both, :] = near
            if d == 0:
                halo_out[i, half * both :, :] = (field - near.astype(F32)).astype(BF16)

    for fetch in fetches[1:4]:
        fetch.wait()
    meta[me, 0:STEPS, :] = dest_ref[...]
    meta[me, STEPS : 2 * STEPS, :] = jnp.zeros((STEPS, cols), jnp.int32)
    for s in range(STEPS):
        index = bound_ref[s : s + 1, :]
        at_col = lax.rem(lax.rem(index, width) + shift_ref[s] + width, width)
        meta[me, STEPS + s : STEPS + s + 1, 0:nb] = (index // width) * width + at_col

    pl.semaphore_wait(barrier, tiles)

    pending = []

    def start(copy):
        copy.start()
        pending.append(copy)

    def halo_pair(i, tile):
        return (
            rcopy(halo_out.at[i], halo_in.at[i], halo_s.at[i], halo_r.at[i], tile),
            rcopy(terrain_ref, terr_in.at[i], terr_s.at[i], terr_r.at[i], tile),
        )

    has = (me < tiles - 1, me > 0)
    to = (lax.rem(me + 1, tiles), lax.rem(me + tiles - 1, tiles))
    for i in range(2):
        @pl.when(has[i])
        def _():
            for copy in halo_pair(i, to[i]):
                copy.start()

    for d in range(1, tiles):
        start(rcopy(meta.at[me], meta.at[me], meta_s.at[d], meta_r.at[d], at(d)))

    for fetch in fetches[4:]:
        fetch.wait()
    for m in range(members):
        zg[my_z, m] = nn(last_ref[...], nest_ref[:, m, :], HI)
        for d in range(1, zs):
            block = zg.at[my_z, m]
            start(rcopy(block, block, z_s.at[m, d], z_r.at[m, d], at(d * PLANE)))

    for d in range(1, tiles):
        rcopy(meta.at[me], meta.at[at(tiles - d)], meta_s.at[d], meta_r.at[d], me).wait_recv()

    t_iota = lax.broadcasted_iota(jnp.int32, (tiles, cols), 0)
    dest = [meta[:, s, :] for s in range(STEPS)]
    dest_tile = [v // cols for v in dest]

    def chase(final):
        tau = jnp.zeros((1, cols), jnp.int32) + final
        sources, slots, firsts = [None] * STEPS, [None] * STEPS, [None] * STEPS
        for s in range(STEPS - 1, -1, -1):
            hit = dest_tile[s] == tau
            tau = jnp.sum(jnp.where(hit, t_iota, 0), axis=0, keepdims=True)
            slots[s] = jnp.sum(jnp.where(hit, dest[s] - dest_tile[s] * cols, 0), axis=0, keepdims=True)
            sources[s] = tau
        return sources, slots

    lane_t = lax.broadcasted_iota(jnp.int32, (tiles, LANES), 1)
    lane_c = lax.broadcasted_iota(jnp.int32, (tiles, cols), 1)
    slot_rows = STEPS * CAPB
    wanted = jnp.zeros((1, LANES), jnp.int32)
    path = None
    for s in range(STEPS - 1, -1, -1):
        hop = one_hot(dest_tile[s][:, 0:1] == lane_t // slot_rows)
        if path is None:
            path = hop
        else:
            step_hop = one_hot(dest_tile[s][:, 0:1] == lane_t)
            above = jnp.concatenate([path, jnp.zeros((LANES - tiles, LANES), BF16)], axis=0)
            path = nn(step_hop, above).astype(BF16)
        cell = meta[:, STEPS + s, :]
        owned = jnp.logical_and(cell // cells == me, lane_c < nb)
        local = lax.rem(cell, cells) + 1
        for k in range(CAPB):
            pick_k = jnp.logical_and(owned, lax.rem(lane_c, CAPB) == k)
            which = jnp.sum(jnp.where(pick_k, local, 0), axis=1, keepdims=True)
            there = jnp.logical_and(path > 0, lax.rem(lane_t, slot_rows) == s * CAPB + k)
            wanted = wanted + jnp.sum(jnp.where(there, which, 0), axis=0, keepdims=True)
    cell_iota = lax.broadcasted_iota(jnp.int32, (cells, LANES), 0)
    requests = one_hot(cell_iota == wanted - 1)

    sources, slots = chase(me)

    q_iota = lax.broadcasted_iota(jnp.int32, (cols, cols), 0)
    j_iota = lax.broadcasted_iota(jnp.int32, (cols, cols), 1)
    relax = jnp.where(j_iota < nb, 1.0 - RELAX_RATE, 1.0)
    moves = [None] * STEPS
    path = None
    for s in range(STEPS - 1, -1, -1):
        hop = jnp.where(slots[s] == q_iota, relax, 0.0).astype(BF16)
        path = hop if path is None else nn(path, hop).astype(BF16)
        moves[s] = path

    def masked(origin, m):
        out = jnp.zeros((padded, cols), F32)
        for z in range(zs):
            out = jnp.where(origin == z * PLANE + my_p, zg[z, m], out)
        return out

    finals = [my_z * PLANE + lax.rem(my_p + d, PLANE) for d in range(PLANE)]
    origins = [sources[0]] + [chase(final)[0][0] for final in finals[1:]]

    def second_leg(m):
        for d in range(1, zs):
            sent = zg.at[my_z, m]
            came = zg.at[lax.rem(my_z + zs - d, zs), m]
            rcopy(sent, came, z_s.at[m, d], z_r.at[m, d], me).wait_recv()
        for d in range(1, PLANE):
            pm[d - 1, m] = masked(origins[d], m)
            start(rcopy(pm.at[d - 1, m], pr.at[d - 1, m], p_s.at[m, d], p_r.at[m, d], finals[d]))

    lane_s = lax.rem(lax.broadcasted_iota(jnp.int32, (both, LANES), 1), slot_rows) // CAPB
    picked = [jnp.zeros((both, LANES), F32)]

    def pick(t):
        field = jnp.concatenate(
            [
                jnp.concatenate(
                    [w[t, half + r, m, EDGE : EDGE + padded, :] for m in range(members)], axis=0
                ).astype(BF16)
                for r in range(rows)
            ],
            axis=1,
        )
        picked[0] = jnp.where(lane_s == t, nn(field, requests), picked[0])

    pick(0)

    def coefficient(terr_row):
        return 1.0 - 4.0 * HORIZ_MIX - 2.0 * VERT_MIX - DRAG_RATE * terr_row.astype(F32) / 3000.0

    def centre_of(r):
        if r < half:
            return coefficient(terr_in[0, rows - half + r : rows - half + r + 1, :])
        if r < half + rows:
            return coefficient(terrain_ref[r - half : r - half + 1, :])
        return coefficient(terr_in[1, r - half - rows : r - half - rows + 1, :])

    def guard(t, r):
        for m in range(members):
            w[t, r, m, EDGE - 1 : EDGE, :] = w[t, r, m, EDGE : EDGE + 1, :]
            w[t, r, m, EDGE + levels : EDGE + levels + 1, :] = w[
                t, r, m, EDGE + levels - 1 : EDGE + levels, :
            ]

    def advance(t, r):
        centre = centre_of(r)
        beyond = None
        if r < half:
            beyond = jnp.where(has[1], 1.0, 0.0)
        elif r >= half + rows:
            beyond = jnp.where(has[0], 1.0, 0.0)
        guard(t, r)
        for m in range(members):
            cur = w[t, r, m, EDGE : EDGE + padded, :]
            up = w[t, r, m, EDGE + 1 : EDGE + 1 + padded, :]
            down = w[t, r, m, EDGE - 1 : EDGE - 1 + padded, :]
            north = w[t, r + 1, m, EDGE : EDGE + padded, :]
            south = w[t, r - 1, m, EDGE : EDGE + padded, :]
            sides = (north + south) + (pltpu.roll(cur, 1, axis=1) + pltpu.roll(cur, width - 1, axis=1))
            new = centre * cur + HORIZ_MIX * sides + VERT_MIX * (up + down)
            if beyond is not None:
                new = new * beyond
            if t == STEPS - 1:
                parent_out[pl.ds(m * levels * rows + r - half, levels, stride=rows), :] = new[:levels]
            else:
                w[t + 1, r, m, EDGE : EDGE + padded, :] = new

    for t in range(STEPS - 1):
        for r in range(half + t + 1, half + rows - t - 1):
            advance(t, r)

    second_leg(0)

    def outer(t):
        inner = range(half + t + 1, half + rows - t - 1)
        for r in range(t + 1, tall - t - 1):
            if r not in inner:
                advance(t, r)

    for i in range(2):
        @pl.when(has[1 - i])
        def _():
            for copy in halo_pair(i, me):
                copy.wait_recv()
            for d in range(half):
                row = half - 1 - d if i == 0 else half + rows + d
                came = halo_in[i, d * both : (d + 1) * both, :].astype(F32)
                if d == 0:
                    came = came + halo_in[i, half * both :, :].astype(F32)
                for m in range(members):
                    w[0, row, m, EDGE : EDGE + padded, :] = came[m * padded : (m + 1) * padded]

        @pl.when(jnp.logical_not(has[1 - i]))
        def _():
            terr_in[i] = jnp.zeros((rows, width), jnp.int32)
            for d in range(half):
                row = half - 1 - d if i == 0 else half + rows + d
                for m in range(members):
                    w[0, row, m, EDGE : EDGE + padded, :] = jnp.zeros((padded, width), F32)

    outer(0)
    pick(1)

    second_leg(1)

    for t in range(2, STEPS):
        outer(t - 1)
        pick(t)
    for m in range(members):
        part = picked[0][m * padded : (m + 1) * padded]
        part = jnp.concatenate([part, jnp.zeros((LANES - padded, LANES), F32)], axis=0)
        msg[m] = jnp.transpose(part)

    def rows_of(tile):
        return pl.ds(pl.multiple_of(tile * slot_rows, slot_rows), slot_rows)

    for d in range(1, tiles):
        start(rcopy(msg.at[:, rows_of(at(d))], got.at[:, rows_of(me)], msg_s.at[d], msg_r.at[d], at(d)))
    got[:, rows_of(me), :] = msg[:, rows_of(me), :]

    for r in range(half, half + rows):
        advance(STEPS - 1, r)
    keep = pltpu.make_async_copy(parent_out, parent_hbm, out_s)
    keep.start()

    origin = sources[0]
    for d in range(1, PLANE):
        for m in range(members):
            rcopy(pm.at[d - 1, m], pr.at[d - 1, m], p_s.at[m, d], p_r.at[m, d], me).wait_recv()
    result = []
    for m in range(members):
        block = masked(origin, m)
        for d in range(1, PLANE):
            came = lax.rem(origin, PLANE) == lax.rem(my_p + PLANE - d, PLANE)
            block = jnp.where(came, pr[d - 1, m], block)
        result.append(nt(block, moves[0].astype(F32), HI))

    g_rows = tiles * slot_rows
    lane_1 = lax.broadcasted_iota(jnp.int32, (SUB, LANES), 1)
    row_1 = lax.broadcasted_iota(jnp.int32, (SUB, cols), 0)
    lane_j = lax.broadcasted_iota(jnp.int32, (SUB, cols), 1)
    weight = jnp.zeros((SUB, LANES), F32)
    place = jnp.zeros((SUB, LANES), F32)
    for s in range(STEPS):
        asker = sources[s][:, 0:1]
        cell = jnp.sum(
            jnp.where(t_iota == asker, meta[:, STEPS + s, :], 0), axis=0, keepdims=True
        )
        fed = (cell // cells) * slot_rows + s * CAPB + lax.rem(lane_j, CAPB)
        table = jnp.where(row_1 == 0, 1, fed)
        table = jnp.where(lane_j < nb, table, 0).astype(F32).astype(BF16)
        hot = jnp.where(moves[s] > 0, 1.0, 0.0).astype(BF16)
        here = lane_1 // per == s
        moved = pltpu.roll(nt(table, moves[s])[:, :LANES], s * per, axis=1)
        weight = jnp.where(here, moved, weight)
        moved = pltpu.roll(nt(table, hot)[:, :LANES], s * per, axis=1)
        place = jnp.where(here, moved, place)
    place = place[1:2].astype(jnp.int32)
    g_iota = lax.broadcasted_iota(jnp.int32, (g_rows, LANES), 0)
    takes = jnp.where(g_iota == place, weight[0:1], 0.0).astype(BF16)

    for d in range(1, tiles):
        rcopy(
            msg.at[:, rows_of(me)], got.at[:, rows_of(at(tiles - d))], msg_s.at[d], msg_r.at[d], me
        ).wait_recv()
    entries = [nn(jnp.transpose(got[m]).astype(BF16), takes).astype(BF16) for m in range(members)]
    solved = nn(parts_ref[...], jnp.concatenate(entries, axis=1))
    lane_p = lax.broadcasted_iota(jnp.int32, (padded, LANES), 1)
    for m in range(members):
        added = jnp.zeros((padded, LANES), F32)
        for s in range(STEPS):
            terms = [
                solved[(s * PARTS + part) * padded : (s * PARTS + part + 1) * padded,
                       m * LANES : (m + 1) * LANES]
                for part in range(PARTS)
            ]
            added = jnp.where(lane_p // per == s, terms[0] + (terms[1] + terms[2]), added)
        span = LANES // 2
        while span >= per:
            added = added + pltpu.roll(added, span, axis=1)
            span //= 2
        added = jnp.where(lane_p < per, added, 0.0)
        if cols > LANES:
            added = jnp.concatenate([added, jnp.zeros((padded, cols - LANES), F32)], axis=1)
        full = result[m] + added
        mine[m] = full
        nest_out[:, m, :] = full[:levels]

    pair = rcopy(mine, theirs, mem_s, mem_r, me, 1 - core)
    pair.start()
    pair.wait()
    count = 2 * members
    fields = [mine[m, 0:levels] for m in range(members)]
    fields += [theirs[m, 0:levels] for m in range(members)]
    mean = functools.reduce(lambda a, b: a + b, fields) / count
    mean_out[...] = mean
    var_out[...] = functools.reduce(lambda a, b: a + b, [(f - mean) ** 2 for f in fields]) / count

    keep.wait()
    for copy in pending:
        copy.wait_send()
    for i in range(2):
        @pl.when(has[i])
        def _():
            for copy in halo_pair(i, to[i]):
                copy.wait_send()


def write_out(parent_ref, nest_ref, mean_ref, var_ref, parent_out, nest_out, mean_out, var_out, sems):
    piece = parent_ref.shape[0] // WRITES
    copies = [
        pltpu.make_async_copy(
            parent_ref.at[pl.ds(i * piece, piece)], parent_out.at[pl.ds(i * piece, piece)], sems.at[i]
        )
        for i in range(WRITES)
    ]
    others = ((nest_ref, nest_out), (mean_ref, mean_out), (var_ref, var_out))
    for i, (source, place) in enumerate(others):
        copies.append(pltpu.make_async_copy(source, place, sems.at[WRITES + i]))
    for copy in copies:
        copy.start()
    for copy in copies:
        copy.wait()


def on_device_fused(parent_state, nest_state, terrain, shift_x, boundary_index, reloc_dest):
    members, levels, rows, width = parent_state.shape
    cols = nest_state.shape[2]
    nb = boundary_index.shape[1]
    tiles = lax.axis_size("tile")
    cells = rows * width
    padded = -(-levels // 8) * 8
    zs = tiles // PLANE
    slot_rows = STEPS * CAPB
    mixed = members * levels
    both = members * padded
    dims = (members, levels, rows, width, cols, nb, tiles, cols // (tiles // 2), cells)
    vmem = pl.BlockSpec(memory_space=pltpu.VMEM)
    hbm = pl.BlockSpec(memory_space=pl.ANY)
    dma = pltpu.SemaphoreType.DMA
    last, parts = inverse_powers(levels)
    outs = pl.pallas_call(
        functools.partial(fused, dims),
        out_shape=(
            jax.ShapeDtypeStruct((mixed * rows, width), F32),
            jax.ShapeDtypeStruct((levels, members, cols), F32),
            jax.ShapeDtypeStruct((levels, cols), F32),
            jax.ShapeDtypeStruct((levels, cols), F32),
        ),
        in_specs=[hbm] * 3 + [pl.BlockSpec(memory_space=pltpu.SMEM)] + [hbm] * 4,
        out_specs=(hbm, vmem, vmem, vmem),
        scratch_shapes=[
            pltpu.VMEM((mixed * rows, width), F32),
            pltpu.VMEM((levels, members, cols), F32),
            pltpu.VMEM((rows, width), jnp.int32),
            pltpu.VMEM((STEPS, nb), jnp.int32),
            pltpu.VMEM((STEPS, cols), jnp.int32),
            pltpu.VMEM(last.shape, F32),
            pltpu.VMEM(parts.shape, BF16),
            dma((7,)),
            pltpu.VMEM((mixed * rows, width), F32),
            dma,
            pltpu.VMEM((tiles, 2 * STEPS, cols), jnp.int32),
            pltpu.VMEM((2, (rows // 2 + 1) * both, width), BF16),
            pltpu.VMEM((2, (rows // 2 + 1) * both, width), BF16),
            pltpu.VMEM((2, rows, width), jnp.int32),
            pltpu.VMEM((zs, members, padded, cols), F32),
            pltpu.VMEM((PLANE - 1, members, padded, cols), F32),
            pltpu.VMEM((PLANE - 1, members, padded, cols), F32),
            pltpu.VMEM((STEPS, 2 * rows, members, padded + 2 * EDGE, width), F32),
            pltpu.VMEM((members, tiles * slot_rows, LANES), F32),
            pltpu.VMEM((members, tiles * slot_rows, LANES), F32),
            pltpu.VMEM((members, padded, cols), F32),
            pltpu.VMEM((members, padded, cols), F32),
            dma((tiles,)), dma((tiles,)),
            dma((2,)), dma((2,)), dma((2,)), dma((2,)),
            dma((members, zs)), dma((members, zs)),
            dma((members, PLANE)), dma((members, PLANE)),
            dma((tiles,)), dma((tiles,)),
            dma, dma,
        ],
        compiler_params=pltpu.CompilerParams(
            collective_id=0, has_side_effects=True, vmem_limit_bytes=62 * 1024 * 1024
        ),
    )(
        parent_state.reshape(mixed * rows, width),
        jnp.transpose(nest_state, (1, 0, 2)), terrain, shift_x, boundary_index, reloc_dest,
        jnp.asarray(last), jnp.asarray(parts),
    )
    outs = pl.pallas_call(
        write_out,
        out_shape=(
            jax.ShapeDtypeStruct((mixed * rows, width), F32),
            jax.ShapeDtypeStruct((levels, members, cols), F32),
            jax.ShapeDtypeStruct((levels, cols), F32),
            jax.ShapeDtypeStruct((levels, cols), F32),
        ),
        in_specs=[hbm] * 4,
        out_specs=(hbm,) * 4,
        scratch_shapes=[dma((WRITES + 3,))],
        compiler_params=pltpu.CompilerParams(vmem_limit_bytes=62 * 1024 * 1024),
    )(*outs)
    nest_field = jnp.transpose(outs[1], (1, 0, 2))
    return (outs[0].reshape(parent_state.shape), nest_field, outs[2], outs[3])


def fits_one_plane_split(mesh, parent, nest, bound):
    tiles = mesh.shape["tile"]
    cols = nest[2] // tiles
    return (
        tiles == PLANE * PLANE
        and mesh.shape["member"] == 2
        and bound[1] // tiles <= cols // (tiles // 2)
        and nest[1] <= LANES
        and nest[0] == 4
        and parent[2] // tiles == 2 * STEPS
        and parent[3] == LANES
        and cols % LANES == 0
        and STEPS * (cols // (tiles // 2)) == LANES
    )


def solution(mesh):
    in_specs = (
        P("member", None, "tile", None),
        P("member", None, "tile"),
        P("tile", None),
        P(),
        P(None, "tile"),
        P(None, "tile"),
    )
    out_specs = (
        P("member", None, "tile", None),
        P("member", None, "tile"),
        P(None, "tile"),
        P(None, "tile"),
    )

    def whole(parent_state, nest_state, terrain, shift_x, boundary_index, reloc_dest):
        fits = fits_one_plane_split(mesh, parent_state.shape, nest_state.shape, boundary_index.shape)
        return jax.shard_map(
            on_device_fused if fits else on_device,
            mesh=mesh, in_specs=in_specs, out_specs=out_specs, check_vma=False,
        )(parent_state, nest_state, terrain, shift_x, boundary_index, reloc_dest)

    return whole
```

```python
import functools

import jax
import jax.numpy as jnp
import numpy as np
from jax import lax
from jax.experimental import pallas as pl
from jax.experimental.pallas import tpu as pltpu
from jax.sharding import PartitionSpec as P

CAPB = 2
STEPS = 4


HORIZ_MIX = 0.15
VERT_MIX = 0.1
DRAG_RATE = 0.1
RELAX_RATE = 0.5
IMPLICIT_MIX = 0.8


def with_halo(block, sides, width):
    for axis, dim in sides:
        count = lax.axis_size(axis)
        forward = [(i, i + 1) for i in range(count - 1)]
        backward = [(target, source) for source, target in forward]
        low = lax.ppermute(
            lax.slice_in_dim(block, block.shape[dim] - width, None, axis=dim), axis, forward
        )
        high = lax.ppermute(lax.slice_in_dim(block, 0, width, axis=dim), axis, backward)
        block = jnp.concatenate([low, block, high], axis=dim)
    return block


def parent_update(parent, damping):
    padded = with_halo(parent, (("tile", 2),), 1)
    north_row = padded[:, :, 2:, :]
    south_row = padded[:, :, :-2, :]
    east_cell = jnp.roll(parent, -1, axis=3)
    west_cell = jnp.roll(parent, 1, axis=3)
    upper_level = jnp.concatenate([parent[:, 1:], parent[:, -1:]], axis=1)
    lower_level = jnp.concatenate([parent[:, :1], parent[:, :-1]], axis=1)
    return (
        parent
        + HORIZ_MIX * (north_row + south_row + east_cell + west_cell - 4.0 * parent)
        + VERT_MIX * (upper_level + lower_level - 2.0 * parent)
        - damping * parent
    )


def implicit_column(column_field):
    levels = column_field.shape[1]
    pivots = []
    cprime = []
    previous = 0.0
    for level in range(levels):
        neighbours = (1 if level > 0 else 0) + (1 if level < levels - 1 else 0)
        diagonal = 1.0 + IMPLICIT_MIX * neighbours
        pivot = diagonal - IMPLICIT_MIX * previous if level > 0 else diagonal
        previous = IMPLICIT_MIX / pivot
        pivots.append(pivot)
        cprime.append(previous)
    sweep = []
    forward = None
    for level in range(levels):
        source = column_field[:, level]
        if level > 0:
            source = source + IMPLICIT_MIX * forward
        forward = source / pivots[level]
        sweep.append(forward)
    result = [None] * levels
    result[levels - 1] = sweep[levels - 1]
    for level in range(levels - 2, -1, -1):
        result[level] = sweep[level] + cprime[level] * result[level + 1]
    return jnp.stack(result, axis=1)


def locate(indices, shift_by, row_width, tile_cells):
    rows_at = indices // row_width
    cols_at = jnp.mod(indices % row_width + shift_by, row_width)
    moved = rows_at * row_width + cols_at
    return (moved // tile_cells, moved % tile_cells)


def on_device(parent_state, nest_state, terrain, shift_x, boundary_index, reloc_dest):
    members, levels, rows_here, row_width = parent_state.shape
    columns_here = nest_state.shape[2]
    tile_count = lax.axis_size("tile")
    tile_cells = rows_here * row_width
    boundary_here = boundary_index.shape[1]
    owners = boundary_here // CAPB
    mixed = members * levels
    groups = tile_count // 2
    per_peer = columns_here // groups
    damping = DRAG_RATE * terrain.astype(jnp.float32) / 3000.0
    parent = parent_state
    nest_field = nest_state
    for step_no in range(STEPS):
        flat_parent = parent.astype(jnp.bfloat16).reshape(mixed, tile_cells)
        offset = shift_x[step_no]
        owner_of, local_of = locate(boundary_index[step_no], offset, row_width, tile_cells)
        owner_runs = owner_of.reshape(owners, CAPB)[:, 0]
        local_runs = local_of.reshape(owners, CAPB)
        requests_out = jnp.zeros((tile_count, CAPB), jnp.int32).at[owner_runs].set(local_runs)
        values = jnp.transpose(
            jnp.take(
                flat_parent,
                lax.all_to_all(requests_out, "tile", split_axis=0, concat_axis=0, tiled=True),
                axis=1,
            ),
            (1, 2, 0),
        )
        received = lax.all_to_all(values, "tile", split_axis=0, concat_axis=0, tiled=True)
        edge_values = received[owner_runs].reshape(boundary_here, mixed)
        edge_values = (
            jnp.transpose(edge_values).astype(jnp.float32).reshape(members, levels, boundary_here)
        )
        edge_cols = nest_field[:, :, :boundary_here]
        edge_cols = edge_cols + RELAX_RATE * (edge_values - edge_cols)
        nest_field = jnp.concatenate([edge_cols, nest_field[:, :, boundary_here:]], axis=2)
        nest_field = implicit_column(nest_field)
        targets = reloc_dest[step_no].reshape(groups, per_peer)
        target_tile = targets[:, 0] // columns_here
        slots = targets % columns_here
        values_out = jnp.transpose(nest_field.reshape(mixed, groups, per_peer), (1, 2, 0))
        send_values = (
            jnp.zeros((tile_count, per_peer, mixed), jnp.float32).at[target_tile].set(values_out)
        )
        send_slots = (
            jnp.full((tile_count, per_peer), columns_here, jnp.int32).at[target_tile].set(slots)
        )
        got_values, got_slots = (
            lax.all_to_all(send_values, "tile", split_axis=0, concat_axis=0, tiled=True),
            lax.all_to_all(send_slots, "tile", split_axis=0, concat_axis=0, tiled=True),
        )
        placed = (
            jnp.zeros((columns_here, mixed), jnp.float32)
            .at[got_slots.reshape(-1)]
            .set(got_values.reshape(-1, mixed), mode="drop")
        )
        nest_field = jnp.transpose(placed).reshape(members, levels, columns_here)
        parent = parent_update(parent, damping)
    ensemble = members * lax.axis_size("member")
    totals = lax.psum(jnp.sum(nest_field, axis=0), "member")
    mean_field = totals / ensemble
    spread_sum = lax.psum(jnp.sum((nest_field - mean_field) ** 2, axis=0), "member")
    variance = spread_sum / ensemble
    return (parent, nest_field, mean_field, variance)


MESH = pl.DeviceIdType.MESH
F32 = jnp.float32
BF16 = jnp.bfloat16
HI = lax.Precision.HIGHEST
PLANE = 4
LANES = 128
PARTS = 3
SUB = 16
EDGE = 8
WRITES = 2


def inverse_powers(levels):
    a = np.zeros((levels, levels))
    for level in range(levels):
        a[level, level] = 1.0
        for other in (level - 1, level + 1):
            if 0 <= other < levels:
                a[level, level] += IMPLICIT_MIX
                a[level, other] = -IMPLICIT_MIX
    inv = np.linalg.inv(a)
    padded = -(-levels // 8) * 8
    parts = np.zeros((STEPS, PARTS, padded, LANES), jnp.bfloat16)
    power = np.eye(levels)
    for k in range(STEPS):
        power = power @ inv
        rest = power
        for part in range(PARTS):
            piece = rest.astype(np.float32).astype(jnp.bfloat16)
            parts[STEPS - 1 - k, part, :levels, :levels] = piece
            rest = rest - piece.astype(np.float64)
    last = np.zeros((padded, levels), np.float32)
    last[:levels] = power
    return last, parts.reshape(STEPS * PARTS * padded, LANES)


def nn(a, b, precision=None):
    return lax.dot_general(
        a, b, (((1,), (0,)), ((), ())), preferred_element_type=F32, precision=precision
    )


def nt(a, b, precision=None):
    return lax.dot_general(
        a, b, (((1,), (1,)), ((), ())), preferred_element_type=F32, precision=precision
    )


def one_hot(mask):
    return jnp.where(mask, 1.0, 0.0).astype(BF16)


def fused(
    dims,
    parent_in, nest_in, terrain_in, shift_ref, bound_in, dest_in, last_in, parts_in,
    parent_hbm, nest_out, mean_out, var_out,
    parent_ref, nest_ref, terrain_ref, bound_ref, dest_ref, last_ref, parts_ref, in_s,
    parent_out, out_s,
    meta, halo_out, halo_in, terr_in, zg, pm, pr, w, msg, got, mine, theirs,
    meta_s, meta_r, halo_s, halo_r, terr_s, terr_r, z_s, z_r, p_s, p_r, msg_s, msg_r, mem_s, mem_r,
):
    members, levels, rows, width, cols, nb, tiles, per, cells = dims
    padded = zg.shape[2]
    zs = tiles // PLANE
    tall = 2 * rows
    half = rows // 2
    me = lax.axis_index("tile")
    core = lax.axis_index("member")
    both = members * padded
    my_p = lax.rem(me, PLANE)
    my_z = me // PLANE

    def rcopy(src, dst, ssem, rsem, tile, member=None):
        return pltpu.make_async_remote_copy(
            src_ref=src, dst_ref=dst, send_sem=ssem, recv_sem=rsem,
            device_id=(core if member is None else member, tile), device_id_type=MESH,
        )

    def at(d):
        return lax.rem(me + d, tiles)

    barrier = pltpu.get_barrier_semaphore()
    for d in range(1, tiles):
        pl.semaphore_signal(barrier, inc=1, device_id=(core, at(d)), device_id_type=MESH)
    pl.semaphore_signal(barrier, inc=1, device_id=(1 - core, me), device_id_type=MESH)

    sources_in = (parent_in, dest_in, bound_in, terrain_in, nest_in, last_in, parts_in)
    places_in = (parent_ref, dest_ref, bound_ref, terrain_ref, nest_ref, last_ref, parts_ref)
    fetches = [
        pltpu.make_async_copy(a, b, in_s.at[i])
        for i, (a, b) in enumerate(zip(sources_in, places_in))
    ]
    for fetch in fetches:
        fetch.start()

    tail = jnp.zeros((w.shape[3] - EDGE - padded + EDGE, width), F32)
    for t in range(STEPS):
        for r in range(tall):
            for m in range(members):
                w[t, r, m, padded:, :] = tail
    fetches[0].wait()
    for r in range(rows):
        for m in range(members):
            w[0, half + r, m, EDGE : EDGE + levels, :] = parent_ref[
                pl.ds(m * levels * rows + r, levels, stride=rows), :
            ]
    for i in range(2):
        for d in range(half):
            row = half + (rows - 1 - d if i == 0 else d)
            field = jnp.concatenate(
                [w[0, row, m, EDGE : EDGE + padded, :] for m in range(members)], axis=0
            )
            near = field.astype(BF16)
            halo_out[i, d * both : (d + 1) * both, :] = near
            if d == 0:
                halo_out[i, half * both :, :] = (field - near.astype(F32)).astype(BF16)

    for fetch in fetches[1:4]:
        fetch.wait()
    meta[me, 0:STEPS, :] = dest_ref[...]
    meta[me, STEPS : 2 * STEPS, :] = jnp.zeros((STEPS, cols), jnp.int32)
    for s in range(STEPS):
        index = bound_ref[s : s + 1, :]
        at_col = lax.rem(lax.rem(index, width) + shift_ref[s] + width, width)
        meta[me, STEPS + s : STEPS + s + 1, 0:nb] = (index // width) * width + at_col

    pl.semaphore_wait(barrier, tiles)

    pending = []

    def start(copy):
        copy.start()
        pending.append(copy)

    def halo_pair(i, tile):
        return (
            rcopy(halo_out.at[i], halo_in.at[i], halo_s.at[i], halo_r.at[i], tile),
            rcopy(terrain_ref, terr_in.at[i], terr_s.at[i], terr_r.at[i], tile),
        )

    has = (me < tiles - 1, me > 0)
    to = (lax.rem(me + 1, tiles), lax.rem(me + tiles - 1, tiles))
    for i in range(2):
        @pl.when(has[i])
        def _():
            for copy in halo_pair(i, to[i]):
                copy.start()

    for d in range(1, tiles):
        start(rcopy(meta.at[me], meta.at[me], meta_s.at[d], meta_r.at[d], at(d)))

    for fetch in fetches[4:]:
        fetch.wait()
    for m in range(members):
        zg[my_z, m] = nn(last_ref[...], nest_ref[:, m, :], HI)
        for d in range(1, zs):
            block = zg.at[my_z, m]
            start(rcopy(block, block, z_s.at[m, d], z_r.at[m, d], at(d * PLANE)))

    for d in range(1, tiles):
        rcopy(meta.at[me], meta.at[at(tiles - d)], meta_s.at[d], meta_r.at[d], me).wait_recv()

    t_iota = lax.broadcasted_iota(jnp.int32, (tiles, cols), 0)
    dest = [meta[:, s, :] for s in range(STEPS)]
    dest_tile = [v // cols for v in dest]

    def chase(final):
        tau = jnp.zeros((1, cols), jnp.int32) + final
        sources, slots, firsts = [None] * STEPS, [None] * STEPS, [None] * STEPS
        for s in range(STEPS - 1, -1, -1):
            hit = dest_tile[s] == tau
            tau = jnp.sum(jnp.where(hit, t_iota, 0), axis=0, keepdims=True)
            slots[s] = jnp.sum(jnp.where(hit, dest[s] - dest_tile[s] * cols, 0), axis=0, keepdims=True)
            sources[s] = tau
        return sources, slots

    lane_t = lax.broadcasted_iota(jnp.int32, (tiles, LANES), 1)
    lane_c = lax.broadcasted_iota(jnp.int32, (tiles, cols), 1)
    slot_rows = STEPS * CAPB
    wanted = jnp.zeros((1, LANES), jnp.int32)
    path = None
    for s in range(STEPS - 1, -1, -1):
        hop = one_hot(dest_tile[s][:, 0:1] == lane_t // slot_rows)
        if path is None:
            path = hop
        else:
            step_hop = one_hot(dest_tile[s][:, 0:1] == lane_t)
            above = jnp.concatenate([path, jnp.zeros((LANES - tiles, LANES), BF16)], axis=0)
            path = nn(step_hop, above).astype(BF16)
        cell = meta[:, STEPS + s, :]
        owned = jnp.logical_and(cell // cells == me, lane_c < nb)
        local = lax.rem(cell, cells) + 1
        for k in range(CAPB):
            pick_k = jnp.logical_and(owned, lax.rem(lane_c, CAPB) == k)
            which = jnp.sum(jnp.where(pick_k, local, 0), axis=1, keepdims=True)
            there = jnp.logical_and(path > 0, lax.rem(lane_t, slot_rows) == s * CAPB + k)
            wanted = wanted + jnp.sum(jnp.where(there, which, 0), axis=0, keepdims=True)
    cell_iota = lax.broadcasted_iota(jnp.int32, (cells, LANES), 0)
    requests = one_hot(cell_iota == wanted - 1)

    sources, slots = chase(me)

    q_iota = lax.broadcasted_iota(jnp.int32, (cols, cols), 0)
    j_iota = lax.broadcasted_iota(jnp.int32, (cols, cols), 1)
    relax = jnp.where(j_iota < nb, 1.0 - RELAX_RATE, 1.0)
    moves = [None] * STEPS
    path = None
    for s in range(STEPS - 1, -1, -1):
        hop = jnp.where(slots[s] == q_iota, relax, 0.0).astype(BF16)
        path = hop if path is None else nn(path, hop).astype(BF16)
        moves[s] = path

    def masked(origin, m):
        out = jnp.zeros((padded, cols), F32)
        for z in range(zs):
            out = jnp.where(origin == z * PLANE + my_p, zg[z, m], out)
        return out

    finals = [my_z * PLANE + lax.rem(my_p + d, PLANE) for d in range(PLANE)]
    origins = [sources[0]] + [chase(final)[0][0] for final in finals[1:]]

    def second_leg(m):
        for d in range(1, zs):
            sent = zg.at[my_z, m]
            came = zg.at[lax.rem(my_z + zs - d, zs), m]
            rcopy(sent, came, z_s.at[m, d], z_r.at[m, d], me).wait_recv()
        for d in range(1, PLANE):
            pm[d - 1, m] = masked(origins[d], m)
            start(rcopy(pm.at[d - 1, m], pr.at[d - 1, m], p_s.at[m, d], p_r.at[m, d], finals[d]))

    lane_s = lax.rem(lax.broadcasted_iota(jnp.int32, (both, LANES), 1), slot_rows) // CAPB
    picked = [jnp.zeros((both, LANES), F32)]

    def pick(t):
        field = jnp.concatenate(
            [
                jnp.concatenate(
                    [w[t, half + r, m, EDGE : EDGE + padded, :] for m in range(members)], axis=0
                ).astype(BF16)
                for r in range(rows)
            ],
            axis=1,
        )
        picked[0] = jnp.where(lane_s == t, nn(field, requests), picked[0])

    pick(0)

    def coefficient(terr_row):
        return 1.0 - 4.0 * HORIZ_MIX - 2.0 * VERT_MIX - DRAG_RATE * terr_row.astype(F32) / 3000.0

    def centre_of(r):
        if r < half:
            return coefficient(terr_in[0, rows - half + r : rows - half + r + 1, :])
        if r < half + rows:
            return coefficient(terrain_ref[r - half : r - half + 1, :])
        return coefficient(terr_in[1, r - half - rows : r - half - rows + 1, :])

    def guard(t, r):
        for m in range(members):
            w[t, r, m, EDGE - 1 : EDGE, :] = w[t, r, m, EDGE : EDGE + 1, :]
            w[t, r, m, EDGE + levels : EDGE + levels + 1, :] = w[
                t, r, m, EDGE + levels - 1 : EDGE + levels, :
            ]

    def advance(t, r):
        centre = centre_of(r)
        beyond = None
        if r < half:
            beyond = jnp.where(has[1], 1.0, 0.0)
        elif r >= half + rows:
            beyond = jnp.where(has[0], 1.0, 0.0)
        guard(t, r)
        for m in range(members):
            cur = w[t, r, m, EDGE : EDGE + padded, :]
            up = w[t, r, m, EDGE + 1 : EDGE + 1 + padded, :]
            down = w[t, r, m, EDGE - 1 : EDGE - 1 + padded, :]
            north = w[t, r + 1, m, EDGE : EDGE + padded, :]
            south = w[t, r - 1, m, EDGE : EDGE + padded, :]
            sides = (north + south) + (pltpu.roll(cur, 1, axis=1) + pltpu.roll(cur, width - 1, axis=1))
            new = centre * cur + HORIZ_MIX * sides + VERT_MIX * (up + down)
            if beyond is not None:
                new = new * beyond
            if t == STEPS - 1:
                parent_out[pl.ds(m * levels * rows + r - half, levels, stride=rows), :] = new[:levels]
            else:
                w[t + 1, r, m, EDGE : EDGE + padded, :] = new

    for t in range(STEPS - 1):
        for r in range(half + t + 1, half + rows - t - 1):
            advance(t, r)

    second_leg(0)

    def outer(t):
        inner = range(half + t + 1, half + rows - t - 1)
        for r in range(t + 1, tall - t - 1):
            if r not in inner:
                advance(t, r)

    for i in range(2):
        @pl.when(has[1 - i])
        def _():
            for copy in halo_pair(i, me):
                copy.wait_recv()
            for d in range(half):
                row = half - 1 - d if i == 0 else half + rows + d
                came = halo_in[i, d * both : (d + 1) * both, :].astype(F32)
                if d == 0:
                    came = came + halo_in[i, half * both :, :].astype(F32)
                for m in range(members):
                    w[0, row, m, EDGE : EDGE + padded, :] = came[m * padded : (m + 1) * padded]

        @pl.when(jnp.logical_not(has[1 - i]))
        def _():
            terr_in[i] = jnp.zeros((rows, width), jnp.int32)
            for d in range(half):
                row = half - 1 - d if i == 0 else half + rows + d
                for m in range(members):
                    w[0, row, m, EDGE : EDGE + padded, :] = jnp.zeros((padded, width), F32)

    outer(0)
    pick(1)

    second_leg(1)

    for t in range(2, STEPS):
        outer(t - 1)
        pick(t)
    for m in range(members):
        part = picked[0][m * padded : (m + 1) * padded]
        part = jnp.concatenate([part, jnp.zeros((LANES - padded, LANES), F32)], axis=0)
        msg[m] = jnp.transpose(part)

    def rows_of(tile):
        return pl.ds(pl.multiple_of(tile * slot_rows, slot_rows), slot_rows)

    for d in range(1, tiles):
        start(rcopy(msg.at[:, rows_of(at(d))], got.at[:, rows_of(me)], msg_s.at[d], msg_r.at[d], at(d)))
    got[:, rows_of(me), :] = msg[:, rows_of(me), :]

    for r in range(half, half + rows):
        advance(STEPS - 1, r)
    keep = pltpu.make_async_copy(parent_out, parent_hbm, out_s)
    keep.start()

    origin = sources[0]
    for d in range(1, PLANE):
        for m in range(members):
            rcopy(pm.at[d - 1, m], pr.at[d - 1, m], p_s.at[m, d], p_r.at[m, d], me).wait_recv()
    result = []
    for m in range(members):
        block = masked(origin, m)
        for d in range(1, PLANE):
            came = lax.rem(origin, PLANE) == lax.rem(my_p + PLANE - d, PLANE)
            block = jnp.where(came, pr[d - 1, m], block)
        result.append(nt(block, moves[0].astype(F32), HI))

    g_rows = tiles * slot_rows
    lane_1 = lax.broadcasted_iota(jnp.int32, (SUB, LANES), 1)
    row_1 = lax.broadcasted_iota(jnp.int32, (SUB, cols), 0)
    lane_j = lax.broadcasted_iota(jnp.int32, (SUB, cols), 1)
    weight = jnp.zeros((SUB, LANES), F32)
    place = jnp.zeros((SUB, LANES), F32)
    for s in range(STEPS):
        asker = sources[s][:, 0:1]
        cell = jnp.sum(
            jnp.where(t_iota == asker, meta[:, STEPS + s, :], 0), axis=0, keepdims=True
        )
        fed = (cell // cells) * slot_rows + s * CAPB + lax.rem(lane_j, CAPB)
        table = jnp.where(row_1 == 0, 1, fed)
        table = jnp.where(lane_j < nb, table, 0).astype(F32).astype(BF16)
        hot = jnp.where(moves[s] > 0, 1.0, 0.0).astype(BF16)
        here = lane_1 // per == s
        moved = pltpu.roll(nt(table, moves[s])[:, :LANES], s * per, axis=1)
        weight = jnp.where(here, moved, weight)
        moved = pltpu.roll(nt(table, hot)[:, :LANES], s * per, axis=1)
        place = jnp.where(here, moved, place)
    place = place[1:2].astype(jnp.int32)
    g_iota = lax.broadcasted_iota(jnp.int32, (g_rows, LANES), 0)
    takes = jnp.where(g_iota == place, weight[0:1], 0.0).astype(BF16)

    for d in range(1, tiles):
        rcopy(
            msg.at[:, rows_of(me)], got.at[:, rows_of(at(tiles - d))], msg_s.at[d], msg_r.at[d], me
        ).wait_recv()
    entries = [nn(jnp.transpose(got[m]).astype(BF16), takes).astype(BF16) for m in range(members)]
    solved = nn(parts_ref[...], jnp.concatenate(entries, axis=1))
    lane_p = lax.broadcasted_iota(jnp.int32, (padded, LANES), 1)
    for m in range(members):
        added = jnp.zeros((padded, LANES), F32)
        for s in range(STEPS):
            terms = [
                solved[(s * PARTS + part) * padded : (s * PARTS + part + 1) * padded,
                       m * LANES : (m + 1) * LANES]
                for part in range(PARTS)
            ]
            added = jnp.where(lane_p // per == s, terms[0] + (terms[1] + terms[2]), added)
        span = LANES // 2
        while span >= per:
            added = added + pltpu.roll(added, span, axis=1)
            span //= 2
        added = jnp.where(lane_p < per, added, 0.0)
        if cols > LANES:
            added = jnp.concatenate([added, jnp.zeros((padded, cols - LANES), F32)], axis=1)
        full = result[m] + added
        mine[m] = full
        nest_out[:, m, :] = full[:levels]

    pair = rcopy(mine, theirs, mem_s, mem_r, me, 1 - core)
    pair.start()
    pair.wait()
    count = 2 * members
    fields = [mine[m, 0:levels] for m in range(members)]
    fields += [theirs[m, 0:levels] for m in range(members)]
    mean = functools.reduce(lambda a, b: a + b, fields) / count
    mean_out[...] = mean
    var_out[...] = functools.reduce(lambda a, b: a + b, [(f - mean) ** 2 for f in fields]) / count

    keep.wait()
    for copy in pending:
        copy.wait_send()
    for i in range(2):
        @pl.when(has[i])
        def _():
            for copy in halo_pair(i, to[i]):
                copy.wait_send()


def write_out(parent_ref, nest_ref, mean_ref, var_ref, parent_out, nest_out, mean_out, var_out, sems):
    piece = parent_ref.shape[0] // WRITES
    copies = [
        pltpu.make_async_copy(
            parent_ref.at[pl.ds(i * piece, piece)], parent_out.at[pl.ds(i * piece, piece)], sems.at[i]
        )
        for i in range(WRITES)
    ]
    others = ((nest_ref, nest_out), (mean_ref, mean_out), (var_ref, var_out))
    for i, (source, place) in enumerate(others):
        copies.append(pltpu.make_async_copy(source, place, sems.at[WRITES + i]))
    for copy in copies:
        copy.start()
    for copy in copies:
        copy.wait()


def on_device_fused(parent_state, nest_state, terrain, shift_x, boundary_index, reloc_dest):
    members, levels, rows, width = parent_state.shape
    cols = nest_state.shape[2]
    nb = boundary_index.shape[1]
    tiles = lax.axis_size("tile")
    cells = rows * width
    padded = -(-levels // 8) * 8
    zs = tiles // PLANE
    slot_rows = STEPS * CAPB
    mixed = members * levels
    both = members * padded
    dims = (members, levels, rows, width, cols, nb, tiles, cols // (tiles // 2), cells)
    vmem = pl.BlockSpec(memory_space=pltpu.VMEM)
    hbm = pl.BlockSpec(memory_space=pl.ANY)
    dma = pltpu.SemaphoreType.DMA
    last, parts = inverse_powers(levels)
    outs = pl.pallas_call(
        functools.partial(fused, dims),
        out_shape=(
            jax.ShapeDtypeStruct((mixed * rows, width), F32),
            jax.ShapeDtypeStruct((levels, members, cols), F32),
            jax.ShapeDtypeStruct((levels, cols), F32),
            jax.ShapeDtypeStruct((levels, cols), F32),
        ),
        in_specs=[hbm] * 3 + [pl.BlockSpec(memory_space=pltpu.SMEM)] + [hbm] * 4,
        out_specs=(hbm, vmem, vmem, vmem),
        scratch_shapes=[
            pltpu.VMEM((mixed * rows, width), F32),
            pltpu.VMEM((levels, members, cols), F32),
            pltpu.VMEM((rows, width), jnp.int32),
            pltpu.VMEM((STEPS, nb), jnp.int32),
            pltpu.VMEM((STEPS, cols), jnp.int32),
            pltpu.VMEM(last.shape, F32),
            pltpu.VMEM(parts.shape, BF16),
            dma((7,)),
            pltpu.VMEM((mixed * rows, width), F32),
            dma,
            pltpu.VMEM((tiles, 2 * STEPS, cols), jnp.int32),
            pltpu.VMEM((2, (rows // 2 + 1) * both, width), BF16),
            pltpu.VMEM((2, (rows // 2 + 1) * both, width), BF16),
            pltpu.VMEM((2, rows, width), jnp.int32),
            pltpu.VMEM((zs, members, padded, cols), F32),
            pltpu.VMEM((PLANE - 1, members, padded, cols), F32),
            pltpu.VMEM((PLANE - 1, members, padded, cols), F32),
            pltpu.VMEM((STEPS, 2 * rows, members, padded + 2 * EDGE, width), F32),
            pltpu.VMEM((members, tiles * slot_rows, LANES), F32),
            pltpu.VMEM((members, tiles * slot_rows, LANES), F32),
            pltpu.VMEM((members, padded, cols), F32),
            pltpu.VMEM((members, padded, cols), F32),
            dma((tiles,)), dma((tiles,)),
            dma((2,)), dma((2,)), dma((2,)), dma((2,)),
            dma((members, zs)), dma((members, zs)),
            dma((members, PLANE)), dma((members, PLANE)),
            dma((tiles,)), dma((tiles,)),
            dma, dma,
        ],
        compiler_params=pltpu.CompilerParams(
            collective_id=0, has_side_effects=True, vmem_limit_bytes=62 * 1024 * 1024
        ),
    )(
        parent_state.reshape(mixed * rows, width),
        jnp.transpose(nest_state, (1, 0, 2)), terrain, shift_x, boundary_index, reloc_dest,
        jnp.asarray(last), jnp.asarray(parts),
    )
    outs = pl.pallas_call(
        write_out,
        out_shape=(
            jax.ShapeDtypeStruct((mixed * rows, width), F32),
            jax.ShapeDtypeStruct((levels, members, cols), F32),
            jax.ShapeDtypeStruct((levels, cols), F32),
            jax.ShapeDtypeStruct((levels, cols), F32),
        ),
        in_specs=[vmem] * 4,
        out_specs=(hbm,) * 4,
        scratch_shapes=[dma((WRITES + 3,))],
        compiler_params=pltpu.CompilerParams(vmem_limit_bytes=62 * 1024 * 1024),
    )(*outs)
    nest_field = jnp.transpose(outs[1], (1, 0, 2))
    return (outs[0].reshape(parent_state.shape), nest_field, outs[2], outs[3])


def fits_one_plane_split(mesh, parent, nest, bound):
    tiles = mesh.shape["tile"]
    cols = nest[2] // tiles
    return (
        tiles == PLANE * PLANE
        and mesh.shape["member"] == 2
        and bound[1] // tiles <= cols // (tiles // 2)
        and nest[1] <= LANES
        and nest[0] == 4
        and parent[2] // tiles == 2 * STEPS
        and parent[3] == LANES
        and cols % LANES == 0
        and STEPS * (cols // (tiles // 2)) == LANES
    )


def solution(mesh):
    in_specs = (
        P("member", None, "tile", None),
        P("member", None, "tile"),
        P("tile", None),
        P(),
        P(None, "tile"),
        P(None, "tile"),
    )
    out_specs = (
        P("member", None, "tile", None),
        P("member", None, "tile"),
        P(None, "tile"),
        P(None, "tile"),
    )

    def whole(parent_state, nest_state, terrain, shift_x, boundary_index, reloc_dest):
        fits = fits_one_plane_split(mesh, parent_state.shape, nest_state.shape, boundary_index.shape)
        return jax.shard_map(
            on_device_fused if fits else on_device,
            mesh=mesh, in_specs=in_specs, out_specs=out_specs, check_vma=False,
        )(parent_state, nest_state, terrain, shift_x, boundary_index, reloc_dest)

    return whole
```
